512 devices in a mesh: seq: 128 (over x, z_hi, y, core), heads: 4 (over z_lo).
Axes of the slice: x: 4, y: 4, z: 16 (z_hi: 4, z_lo: 4; z = z_hi * 4 + z_lo), core: 2. Of those that a mesh axis runs over, the one named last changes fastest.
Arguments:
- x_tiles: bfloat16 [24576, 1536], P('seq'), may hold values from -6 to 6
- x_text: bfloat16 [256, 1536], P('seq'), may hold values from -6 to 6
- w_query: bfloat16 [1536, 1536], P('seq', 'heads'), may hold values from -0.15625 to 0.15625
- w_key: bfloat16 [1536, 1536], P('seq', 'heads'), may hold values from -0.15625 to 0.15625
- w_value: bfloat16 [1536, 1536], P('seq', 'heads'), may hold values from -0.15625 to 0.15625
- w_output: bfloat16 [1536, 1536], P('seq', 'heads'), may hold values from -0.15625 to 0.15625
- q_gain: float32 [1536], P('heads'), may hold values from 0.5 to 8
- k_gain: float32 [1536], P('heads'), may hold values from 0.5 to 8
- text_mask: int32 [256], replicated, may hold values 0 or 1
- windows: int32 [128, 2], replicated, may hold values from 0 to 30, as said below
- grad_out: bfloat16 [24576, 1536], P('seq'), may hold values from -6 to 6
Outputs:
- out_tiles: bfloat16 [24576, 1536], P('seq', 'heads')
- grad_tiles: bfloat16 [24576, 1536], P('seq', 'heads')
The draws below stay inside these ranges and needn't reach their ends.
Inputs may be any that keep to these rules, and one draw needn't show every extreme that they name: windows[t, 0] is tile t's grid row or the one before, and windows[t, 1] its grid column or the one before, so that the window holds tile t and lies in the grid of 4 rows and 32 columns; windows[t, 1] is the same for all tiles of one grid column.
All inputs are finite; a program needn't handle non-finite values.
Results may differ from the reference program's by a relative error of at most 0.019.
Values may be sent and summed in bfloat16 or wider, within the bound.
No kernel may reach another device: no remote copies, remote signals or barrier semaphores. Data moves between devices by JAX's collectives and lax.ppermute only.
A program may use at most 64 MiB of HBM per device.

```python
import jax
import jax.numpy as jnp
from jax import lax

D = 1536
HEADS = 12
HD = 128
TILE_ROWS = 192
TEXT = 256
GB = 32
TILES = 128
ATT = 1536
N_HEADS = 4


def draw_windows(key, part):
    key = jax.random.fold_in(key, 11)
    key_rows, key_cols = jax.random.split(key)
    grid_rows = TILES // GB
    place = jnp.arange(TILES, dtype=jnp.int32)
    row = place // GB
    col = place % GB
    back_rows = jax.random.randint(key_rows, (TILES,), 0, 2).astype(jnp.int32)
    back_cols = jax.random.randint(key_cols, (GB,), 0, 2).astype(jnp.int32)
    col_back = jnp.sum(jnp.where(col[:, None] == jnp.arange(GB, dtype=jnp.int32)[None, :], back_cols[None, :], 0), axis=1)
    row_start = jnp.clip(row - back_rows, 0, grid_rows - 2)
    col_start = jnp.clip(col - col_back, 0, GB - 2)
    return jnp.stack([row_start, col_start], axis=1).astype(jnp.int32)


def gain_values(key, boost):
    key_base, key_heads = jax.random.split(key)
    base = jax.random.uniform(key_base, (HEADS * HD,), jnp.float32, 0.5, 2.0)
    picked = jax.random.uniform(key_heads, (HEADS,), jnp.float32) < 0.25
    factor = jnp.where(picked, boost, 1.0)
    return base * jnp.repeat(factor, HD)


def draw_q_gain(key, part):
    key = jax.random.fold_in(key, 21)
    return gain_values(key, 1.0)


def draw_k_gain(key, part):
    key = jax.random.fold_in(key, 22)
    return gain_values(key, 1.0)


def set_ends(result, stream_key, smallest, largest):
    index_at = [jax.random.randint(jax.random.fold_in(stream_key, axis), (), 0, length) for axis, length in enumerate(result.shape)]
    main_axis = result.shape.index(max(result.shape))
    neighbour = index_at[:main_axis] + [(index_at[main_axis] + 1) % result.shape[main_axis]] + index_at[main_axis + 1:]
    return result.at[tuple(index_at)].set(smallest).at[tuple(neighbour)].set(largest)


def block_levels(stream_key, extent, shards, smallest, largest):
    loudness = 1.0
    for position, blocks in shards:
        steps = jax.random.uniform(jax.random.fold_in(jax.random.fold_in(stream_key, 6), position), (blocks,), jnp.float32, smallest / len(shards), largest / len(shards))
        loudness = loudness * jnp.repeat(jnp.exp(steps), extent[position] // blocks).reshape((-1,) + (1,) * (len(extent) - 1 - position))
    return loudness


def noise(stream_key, shape, deviation, limit, pieces=(), kind=jnp.bfloat16):
    result = deviation * jax.random.normal(stream_key, shape, jnp.float32)
    if pieces:
        result = result * block_levels(stream_key, shape, pieces, -0.22, 0.18)
    return jnp.clip(result, -limit, limit).astype(kind)


def setup_inputs(seed: int = 0) -> dict:
    key_list = jax.random.split(jax.random.key(seed), 12)
    x_tiles = noise(key_list[0], (TILES * TILE_ROWS, D), 1.0, 6.0, ((0, 128),))
    x_text = noise(key_list[1], (TEXT, D), 1.0, 6.0, ((0, 128),))
    w_query = noise(key_list[2], (D, ATT), D ** -0.5, 0.15625, ((0, 128), (1, 4)))
    w_key = noise(key_list[3], (D, ATT), D ** -0.5, 0.15625, ((0, 128), (1, 4)))
    w_value = noise(key_list[4], (D, ATT), D ** -0.5, 0.15625, ((0, 128), (1, 4)))
    w_output = noise(key_list[5], (D, ATT), ATT ** -0.5, 0.15625, ((0, 128), (1, 4)))
    q_gain = draw_q_gain(jax.random.fold_in(key_list[11], 71), 0)
    k_gain = draw_k_gain(jax.random.fold_in(key_list[11], 71), 0)
    text_mask = set_ends((jax.random.randint(key_list[8], (TEXT,), 0, 4) < 3).astype(jnp.int32), jax.random.fold_in(key_list[8], 1), 0, 1)
    windows = draw_windows(jax.random.fold_in(key_list[11], 71), 0)
    grad_out = noise(key_list[10], (TILES * TILE_ROWS, D), 1.0, 6.0, ((0, 128),))
    return dict(x_tiles=x_tiles, x_text=x_text, w_query=w_query, w_key=w_key, w_value=w_value, w_output=w_output, q_gain=q_gain, k_gain=k_gain, text_mask=text_mask, windows=windows, grad_out=grad_out)


def head_norm(values, gain):
    rows = values.shape[0]
    split = values.reshape(rows, -1, HD)
    mean_sq = lax.optimization_barrier(jnp.mean(split * split, axis=-1, keepdims=True))
    scaled = split * lax.rsqrt(mean_sq + 1e-06)
    return scaled.reshape(rows, -1) * gain[None, :]

def softmax_probs(queries, keys, bias):
    scores = jnp.einsum('qhd,khd->hqk', queries.astype(jnp.float32), keys.astype(jnp.float32))
    scores = scores * HD ** (-0.5) + bias[None, None, :]
    top = lax.optimization_barrier(jnp.max(scores, axis=-1, keepdims=True))
    expd = jnp.exp(scores - top)
    return expd / lax.optimization_barrier(jnp.sum(expd, axis=-1, keepdims=True))

def group_sum(parts):
    total = jnp.zeros(parts[0].shape, jnp.float32)
    for piece in parts:
        total = total + lax.optimization_barrier(piece.astype(jnp.bfloat16)).astype(jnp.float32)
    return total.astype(jnp.bfloat16)

def reference(x_tiles, x_text, w_query, w_key, w_value, w_output, q_gain, k_gain, text_mask, windows, grad_out):
    q = jnp.dot(x_tiles, w_query, preferred_element_type=jnp.float32)
    k = jnp.dot(x_tiles, w_key, preferred_element_type=jnp.float32)
    v = jnp.dot(x_tiles, w_value, preferred_element_type=jnp.float32)
    text_k = jnp.dot(x_text, w_key, preferred_element_type=jnp.float32)
    text_v = jnp.dot(x_text, w_value, preferred_element_type=jnp.float32)
    qn = head_norm(q, q_gain).astype(jnp.bfloat16)
    kn = head_norm(k, k_gain).astype(jnp.bfloat16)
    vb = v.astype(jnp.bfloat16)
    text_kn = head_norm(text_k, k_gain).astype(jnp.bfloat16).reshape(TEXT, HEADS, HD)
    text_vb = text_v.astype(jnp.bfloat16).reshape(TEXT, HEADS, HD)
    q_tiles = qn.reshape(TILES, TILE_ROWS, HEADS, HD)
    k_tiles = kn.reshape(TILES, TILE_ROWS, HEADS, HD)
    v_tiles = vb.reshape(TILES, TILE_ROWS, HEADS, HD)
    bias = jnp.concatenate([jnp.zeros((4 * TILE_ROWS,), jnp.float32), jnp.where(text_mask == 1, 0.0, -1e+30).astype(jnp.float32)])
    d_att = jnp.dot(grad_out, w_output, preferred_element_type=jnp.float32).astype(jnp.bfloat16)
    d_att_tiles = d_att.reshape(TILES, TILE_ROWS, HEADS, HD)
    scale = HD ** (-0.5)

    def per_tile(carry, tile):
        acc_k, acc_v = carry
        first_row = windows[tile, 0]
        first_col = windows[tile, 1]
        ids = jnp.stack([first_row * GB + first_col, first_row * GB + first_col + 1, (first_row + 1) * GB + first_col, (first_row + 1) * GB + first_col + 1]).astype(jnp.int32)
        keys = jnp.concatenate([jnp.take(k_tiles, ids, axis=0).reshape(4 * TILE_ROWS, HEADS, HD), text_kn], axis=0)
        vals = jnp.concatenate([jnp.take(v_tiles, ids, axis=0).reshape(4 * TILE_ROWS, HEADS, HD), text_vb], axis=0)
        queries = q_tiles[tile]
        probs = softmax_probs(queries, keys, bias)
        probs_b = probs.astype(jnp.bfloat16)
        attended = jnp.einsum('hqk,khd->qhd', probs_b.astype(jnp.float32), vals.astype(jnp.float32)).astype(jnp.bfloat16)
        d_here = d_att_tiles[tile].astype(jnp.float32)
        dp = jnp.einsum('qhd,khd->hqk', d_here, vals.astype(jnp.float32))
        delta = lax.optimization_barrier(jnp.sum(probs * dp, axis=-1, keepdims=True))
        d_scores = (probs * (dp - delta)).astype(jnp.bfloat16).astype(jnp.float32)
        d_q = jnp.einsum('hqk,khd->qhd', d_scores, keys.astype(jnp.float32)) * scale
        key_terms = jnp.einsum('hqk,qhd->khd', d_scores, queries.astype(jnp.float32)) * scale
        val_terms = jnp.einsum('hqk,qhd->khd', probs_b.astype(jnp.float32), d_here)
        key_terms = key_terms[:4 * TILE_ROWS].reshape(4, TILE_ROWS, HEADS * HD)
        val_terms = val_terms[:4 * TILE_ROWS].reshape(4, TILE_ROWS, HEADS * HD)
        key_terms = lax.optimization_barrier(key_terms.astype(jnp.bfloat16)).astype(jnp.float32)
        val_terms = lax.optimization_barrier(val_terms.astype(jnp.bfloat16)).astype(jnp.float32)
        acc_k = acc_k.at[ids].add(key_terms)
        acc_v = acc_v.at[ids].add(val_terms)
        return ((acc_k, acc_v), (attended.reshape(TILE_ROWS, HEADS * HD), d_q.reshape(TILE_ROWS, HEADS * HD)))
    zeros = jnp.zeros((TILES, TILE_ROWS, HEADS * HD), jnp.float32)
    (acc_k, acc_v), (attended, d_q) = lax.scan(per_tile, (zeros, zeros), jnp.arange(TILES, dtype=jnp.int32))
    attended = attended.reshape(TILES * TILE_ROWS, HEADS * HD)
    d_q = d_q.reshape(TILES * TILE_ROWS, HEADS * HD)
    d_k = acc_k.reshape(TILES * TILE_ROWS, HEADS * HD)
    d_v = acc_v.reshape(TILES * TILE_ROWS, HEADS * HD).astype(jnp.bfloat16)
    pull_q = jax.vjp(lambda a: head_norm(a, q_gain), q)[1]
    pull_k = jax.vjp(lambda a: head_norm(a, k_gain), k)[1]
    d_q_raw = pull_q(d_q)[0].astype(jnp.bfloat16)
    d_k_raw = pull_k(d_k)[0].astype(jnp.bfloat16)
    width = HEADS // N_HEADS * HD
    out_parts = []
    grad_parts = []
    dims = (((1,), (1,)), ((), ()))
    for group in range(N_HEADS):
        low = group * width
        high = low + width
        out_parts.append(lax.dot_general(attended[:, low:high], w_output[:, low:high], dims, preferred_element_type=jnp.float32))
        term = lax.dot_general(d_q_raw[:, low:high], w_query[:, low:high], dims, preferred_element_type=jnp.float32)
        term = term + lax.dot_general(d_k_raw[:, low:high], w_key[:, low:high], dims, preferred_element_type=jnp.float32)
        term = term + lax.dot_general(d_v[:, low:high], w_value[:, low:high], dims, preferred_element_type=jnp.float32)
        grad_parts.append(term)
    return (group_sum(out_parts), group_sum(grad_parts))
```

```python
import functools

import jax
import jax.numpy as jnp
from jax import lax
from jax.experimental import pallas as pl
from jax.experimental.pallas import tpu as pltpu
from jax.sharding import PartitionSpec as P

HD = 128
NH = 3
W = NH * HD
ROWS = 192
TEXT = 256
EPS = 1e-6
SCALE = HD**-0.5
ZH_ORDER = (0, 1, 3, 2)
F32 = jnp.float32
BF16 = jnp.bfloat16
NT = (((1,), (1,)), ((), ()))
TN = (((0,), (0,)), ((), ()))


def place_of(x, zh, y, core):
    return ((x * 4 + zh) * 4 + y) * 2 + core


def all_places():
    return [(x, z, y, c) for x in range(4) for z in range(4) for y in range(4) for c in range(2)]


def seq_move(value, target):
    pairs = []
    for at in all_places():
        to = target(*at)
        if to is not None:
            pairs.append((place_of(*at), place_of(*to)))
    return lax.ppermute(value, "seq", pairs)


def along_x(value, rel):
    return seq_move(value, lambda x, z, y, c: ((x - rel) % 4, z, y, c))


def along_y(value, rel):
    return seq_move(value, lambda x, z, y, c: (x, z, (y - rel) % 4, c))


def across_zh(value, mask):
    return seq_move(value, lambda x, z, y, c: (x, z ^ mask, y, c))


def core_mate(value):
    return seq_move(value, lambda x, z, y, c: (x, z, y, 1 - c))


def next_chip(value):
    def target(x, z, y, c):
        col = (z * 4 + y) * 2 + c
        col = col + 1 if c == 1 else col - 1
        if not 0 <= col < 32:
            return None
        return (x, col // 8, col // 2 % 4, col % 2)

    return seq_move(value, target)


def row_even(value):
    return seq_move(value, lambda x, z, y, c: (x ^ 1, z, y, c))


def row_odd(value):
    return seq_move(value, lambda x, z, y, c: (3 - x, z, y, c) if x in (1, 2) else None)


def dot(a, b, dims=(((1,), (0,)), ((), ()))):
    return lax.dot_general(a, b, dims, preferred_element_type=F32)


def norm_rows(a, gain):
    r = lax.rsqrt(jnp.mean(a * a, axis=-1, keepdims=True) + EPS)
    return a * r * gain


def norm_pull(a, gain, dy):
    r = lax.rsqrt(jnp.mean(a * a, axis=-1, keepdims=True) + EPS)
    t = dy * gain
    return r * t - a * (r * r * r * jnp.mean(t * a, axis=-1, keepdims=True))


def head(h):
    return slice(h * HD, (h + 1) * HD)


def val(h):
    return slice(W + h * HD, W + (h + 1) * HD)


def call(kernel, outs, scratch=(), mib=32, flops=10**9):
    return pl.pallas_call(
        kernel,
        out_shape=outs,
        scratch_shapes=scratch,
        compiler_params=pltpu.CompilerParams(vmem_limit_bytes=mib * 2**20),
        cost_estimate=pl.CostEstimate(flops=flops, bytes_accessed=8 * 10**6, transcendentals=0),
    )


def shape(dims, dtype):
    return jax.ShapeDtypeStruct(dims, dtype)


def kv_kernel(xp, wo, wt, gain, kv, kraw):
    half = wo.shape[0]
    acc = dot(xp[:, :half], wo[...]) + dot(xp[:, half:], wt[...])
    kraw[...] = acc[:, :W]
    for h in range(NH):
        kv[:, head(h)] = norm_rows(acc[:, head(h)], gain[:, head(h)]).astype(BF16)
    kv[:, W:] = acc[:, W:].astype(BF16)


def q_kernel(xp, gp, tp, ao, at, bo, bt, q_gain, k_gain, qraw, qn, d_att, tkv):
    half = bo.shape[0]
    q = dot(xp[:, :half], bo[:, :W]) + dot(xp[:, half:], bt[:, :W])
    qraw[...] = q
    for h in range(NH):
        qn[:, head(h)] = norm_rows(q[:, head(h)], q_gain[:, head(h)]).astype(BF16)
    d = dot(gp[:, :half], bo[:, W:]) + dot(gp[:, half:], bt[:, W:])
    d_att[...] = d.astype(BF16)
    t = dot(tp[:, :half], ao[...]) + dot(tp[:, half:], at[...])
    for h in range(NH):
        tkv[:, head(h)] = norm_rows(t[:, head(h)], k_gain[:, head(h)]).astype(BF16)
    tkv[:, W:] = t[:, W:].astype(BF16)


def attend_kernel(qn, d_att, qraw, q_gain, pair, far, tkv, bias, att, dq, near_t, far_t, keys):
    n = 4 * ROWS
    keys[: 2 * ROWS, :] = pair[...]
    keys[2 * ROWS : n, :] = far[...]
    keys[n:, :] = tkv[...]
    for h in range(NH):
        qh = qn[:, head(h)]
        dh = d_att[:, head(h)]
        kh = keys[:, head(h)]
        vh = keys[:, val(h)]
        s = dot(qh, kh, NT) * SCALE + bias[...]
        e = jnp.exp(s - jnp.max(s, axis=-1, keepdims=True))
        p = e * (1.0 / jnp.sum(e, axis=-1, keepdims=True))
        pb = p.astype(BF16)
        att[:, head(h)] = dot(pb, vh).astype(BF16)
        dp = dot(dh, vh, NT)
        ds = (p * (dp - jnp.sum(p * dp, axis=-1, keepdims=True))).astype(BF16)
        d_q = dot(ds, kh) * SCALE
        dq[:, head(h)] = norm_pull(qraw[:, head(h)], q_gain[:, head(h)], d_q).astype(BF16)
        kt = (dot(ds[:, :n], qh, TN) * SCALE).astype(BF16)
        vt = dot(pb[:, :n], dh, TN).astype(BF16)
        near_t[:, head(h)] = kt[: 2 * ROWS]
        far_t[:, head(h)] = kt[2 * ROWS :]
        near_t[:, val(h)] = vt[: 2 * ROWS]
        far_t[:, val(h)] = vt[2 * ROWS :]


def out_kernel(att, dq, bo, bt, perm, out, gq):
    for j in range(4):
        rows = slice(j * ROWS, (j + 1) * ROWS)
        o = dot(att[...], bo[rows, W:], NT).astype(BF16)
        t = dot(att[...], bt[rows, W:], NT).astype(BF16)
        out[j] = (dot(o, perm[:, :ROWS], NT) + dot(t, perm[:, ROWS:], NT)).astype(BF16)
        gq[0, j] = dot(dq[...], bo[rows, :W], NT)
        gq[1, j] = dot(dq[...], bt[rows, :W], NT)


def grad_kernel(own, in_a, in_b, kraw, k_gain, gq, ao, at, perm, out):
    total = own[...].astype(F32) + in_a[...].astype(F32) + in_b[...].astype(F32)
    parts = [
        norm_pull(kraw[:, head(h)], k_gain[:, head(h)], total[:, head(h)]).astype(BF16)
        for h in range(NH)
    ]
    d = jnp.concatenate(parts + [total[:, W:].astype(BF16)], axis=1)
    for j in range(4):
        rows = slice(j * ROWS, (j + 1) * ROWS)
        o = (gq[0, j] + dot(d, ao[rows, :], NT)).astype(BF16)
        t = (gq[1, j] + dot(d, at[rows, :], NT)).astype(BF16)
        out[j] = (dot(o, perm[:, :ROWS], NT) + dot(t, perm[:, ROWS:], NT)).astype(BF16)


def spread(value, move):
    return [value, move(value, 1), move(value, 2), move(value, 3)]


def head_sum(blocks, x, me):
    def block(to):
        return lax.dynamic_index_in_dim(blocks, (to - x) % 4, 0, keepdims=False)

    total = block(me).astype(F32)
    for by in (1, 2, 3):
        pairs = [(i, (i + by) % 4) for i in range(4)]
        total = total + lax.ppermute(block((me + by) % 4), "heads", pairs).astype(F32)
    return total.astype(BF16)


def per_device(
    x_tiles, x_text, w_query, w_key, w_value, w_output, q_gain, k_gain, text_mask, windows, grad_out
):
    place = lax.axis_index("seq")
    me = lax.axis_index("heads")
    core, y, zh, x = place % 2, place // 2 % 4, place // 8 % 4, place // 32
    col = place % 32
    start = lax.dynamic_slice(windows, (place, jnp.int32(0)), (1, 2))
    want_down = start[0, 0] == x
    want_right = start[0, 1] == col
    use_even = want_down == (x % 2 == 0)
    use_core = want_right == (core == 0)
    q_gain = q_gain[None, :]
    k_gain = k_gain[None, :]

    order = jnp.arange(1536, dtype=jnp.int32)
    r = order % 12
    zr = jnp.array(ZH_ORDER, jnp.int32)[order // 12 % 4] ^ zh
    yr = (order // 48 + y) % 4
    xr = (order // 192 + x) % 4
    cr = (order // 768) ^ core
    natural = place_of(xr, zr, yr, cr) * 12 + r
    perm = (lax.broadcasted_iota(jnp.int32, (1536, 1536), 0) == natural[None, :]).astype(BF16)
    xg = dot(jnp.concatenate([x_tiles, grad_out]), perm).astype(BF16)
    xp, gp = xg[:ROWS], xg[ROWS:]
    first = jnp.concatenate([natural[:ROWS], natural[768 : 768 + ROWS]]) - 384 * x
    small = (lax.broadcasted_iota(jnp.int32, (384, 384), 0) == first[None, :]).astype(BF16)
    t = jnp.arange(TEXT, dtype=jnp.int32)
    tz = jnp.array(ZH_ORDER, jnp.int32)[t // 2 % 4] ^ zh
    token = place_of((t // 32 + x) % 4, tz, (t // 8 + y) % 4, (t // 128) ^ core) * 2 + t % 2
    valid = jnp.sum(
        jnp.where(t[:, None] == token[None, :], text_mask[:, None], 0), axis=0
    )
    bias = jnp.concatenate(
        [jnp.zeros((4 * ROWS,), F32), jnp.where(valid == 1, 0.0, -1e30).astype(F32)]
    )[None, :]

    mine = jnp.concatenate([w_key, w_value, w_query, w_output], axis=1)
    mine = jnp.concatenate([mine, x_text], axis=0)
    two = jnp.stack([mine, across_zh(mine, 1)])
    four = jnp.concatenate([two, across_zh(two, 3)])
    rows = four[:, :12].reshape(48, 1536)
    text = four[:, 12:].reshape(8, 1536)
    a0 = rows[:, :768]
    b0 = jnp.concatenate([rows[:, 768:], text[:, :768], text[:, 768:]], axis=0)
    a1 = jnp.concatenate(spread(a0, along_y))
    ao = jnp.concatenate(spread(a1, along_x))
    at = core_mate(ao)
    b1 = jnp.stack(spread(b0, along_x))
    b2 = jnp.stack(spread(b1, along_y)).transpose(1, 0, 2, 3)
    b3 = core_mate(b2)
    bo = b2[:, :, :48].reshape(768, 768)
    bt = b3[:, :, :48].reshape(768, 768)
    texts = jnp.stack([b2[:, :, 48:], b3[:, :, 48:]]).reshape(2, 4, 4, 2, 8, 768)
    texts = texts.transpose(0, 1, 2, 4, 3, 5).reshape(TEXT, 1536)
    tp = dot(texts, perm).astype(BF16)

    kv, kraw = call(kv_kernel, (shape((ROWS, 768), BF16), shape((ROWS, W), F32)))(
        xp, ao, at, k_gain
    )
    near = jnp.where(use_core, core_mate(kv), next_chip(kv))
    pair = jnp.concatenate([kv, near])
    far = jnp.where(use_even, row_even(pair), row_odd(pair))
    qraw, qn, d_att, tkv = call(
        q_kernel,
        (
            shape((ROWS, W), F32),
            shape((ROWS, W), BF16),
            shape((ROWS, W), BF16),
            shape((TEXT, 768), BF16),
        ),
    )(xp, gp, tp, ao, at, bo, bt, q_gain, k_gain)
    att, dq, near_t, far_t = call(
        attend_kernel,
        (
            shape((ROWS, W), BF16),
            shape((ROWS, W), BF16),
            shape((2 * ROWS, 768), BF16),
            shape((2 * ROWS, 768), BF16),
        ),
        [pltpu.VMEM((1024, 768), BF16)],
    )(qn, d_att, qraw, q_gain, pair, far, tkv, bias)

    zero = jnp.zeros_like(far_t)
    got_even = row_even(jnp.where(use_even, far_t, zero))
    got_odd = row_odd(jnp.where(use_even, zero, far_t))
    summed = (near_t.astype(F32) + got_even.astype(F32) + got_odd.astype(F32)).astype(BF16)
    own_t, side_t = summed[:ROWS], summed[ROWS:]
    zero = jnp.zeros_like(side_t)
    got_core = core_mate(jnp.where(use_core, side_t, zero))
    got_next = next_chip(jnp.where(use_core, zero, side_t))

    out, gq = call(out_kernel, (shape((4, ROWS, W), BF16), shape((2, 4, ROWS, ROWS), F32)))(
        att, dq, bo, bt, small
    )
    out_tiles = head_sum(out, x, me)
    grad = call(grad_kernel, shape((4, ROWS, W), BF16))(
        own_t, got_core, got_next, kraw, k_gain, gq, ao, at, small
    )
    grad_tiles = head_sum(grad, x, me)
    return (out_tiles, grad_tiles)


def solution(mesh):
    in_specs = (
        P("seq", None),
        P("seq", None),
        P("seq", "heads"),
        P("seq", "heads"),
        P("seq", "heads"),
        P("seq", "heads"),
        P("heads"),
        P("heads"),
        P(),
        P(),
        P("seq", None),
    )
    out_specs = (P("seq", "heads"), P("seq", "heads"))
    return jax.shard_map(
        per_device, mesh=mesh, in_specs=in_specs, out_specs=out_specs, check_vma=False
    )
```

```python
import functools

import jax
import jax.numpy as jnp
from jax import lax
from jax.experimental import pallas as pl
from jax.experimental.pallas import tpu as pltpu
from jax.sharding import PartitionSpec as P

HD = 128
NH = 3
W = NH * HD
ROWS = 192
TEXT = 256
EPS = 1e-6
SCALE = HD**-0.5
BLOCK = 56
PART = 4 * BLOCK
F32 = jnp.float32
BF16 = jnp.bfloat16
NT = (((1,), (1,)), ((), ()))
TN = (((0,), (0,)), ((), ()))


def place_of(x, zh, y, core):
    return ((x * 4 + zh) * 4 + y) * 2 + core


def all_places():
    return [(x, z, y, c) for x in range(4) for z in range(4) for y in range(4) for c in range(2)]


def seq_move(value, target):
    pairs = []
    for at in all_places():
        to = target(*at)
        if to is not None:
            pairs.append((place_of(*at), place_of(*to)))
    return lax.ppermute(value, "seq", pairs)


def core_mate(value):
    return seq_move(value, lambda x, z, y, c: (x, z, y, 1 - c))


def next_chip(value):
    def target(x, z, y, c):
        col = (z * 4 + y) * 2 + c
        col = col + 1 if c == 1 else col - 1
        if not 0 <= col < 32:
            return None
        return (x, col // 8, col // 2 % 4, col % 2)

    return seq_move(value, target)


def row_even(value):
    return seq_move(value, lambda x, z, y, c: (x ^ 1, z, y, c))


def row_odd(value):
    return seq_move(value, lambda x, z, y, c: (3 - x, z, y, c) if x in (1, 2) else None)


def give_all(value, groups):
    copies = jnp.broadcast_to(value[None], (len(groups[0]),) + value.shape)
    return lax.all_to_all(copies, "seq", 0, 0, axis_index_groups=groups)


def over_zh(value):
    four = range(4)
    return give_all(
        value,
        [[place_of(x, z, y, c) for z in four] for x in four for y in four for c in range(2)],
    )


def over_xy(value):
    four = range(4)
    return give_all(
        value,
        [[place_of(x, z, y, c) for x in four for y in four] for z in four for c in range(2)],
    )


def dot(a, b, dims=(((1,), (0,)), ((), ()))):
    return lax.dot_general(a, b, dims, preferred_element_type=F32)


def norm_rows(a, gain):
    r = lax.rsqrt(jnp.mean(a * a, axis=-1, keepdims=True) + EPS)
    return a * r * gain


def norm_pull(a, gain, dy):
    r = lax.rsqrt(jnp.mean(a * a, axis=-1, keepdims=True) + EPS)
    t = dy * gain
    return r * t - a * (r * r * r * jnp.mean(t * a, axis=-1, keepdims=True))


def head(h):
    return slice(h * HD, (h + 1) * HD)


def val(h):
    return slice(W + h * HD, W + (h + 1) * HD)


def call(kernel, outs, scratch=(), mib=32, flops=10**9):
    return pl.pallas_call(
        kernel,
        out_shape=outs,
        scratch_shapes=scratch,
        compiler_params=pltpu.CompilerParams(vmem_limit_bytes=mib * 2**20),
        cost_estimate=pl.CostEstimate(flops=flops, bytes_accessed=8 * 10**6, transcendentals=0),
    )


def shape(dims, dtype):
    return jax.ShapeDtypeStruct(dims, dtype)


def project(rows, pick, w, cols):
    acc = None
    for j in range(4):
        xs = dot(rows[:, j * W : (j + 1) * W], pick[...]).astype(BF16)
        term = dot(xs, w[j * PART : (j + 1) * PART, cols])
        acc = term if acc is None else acc + term
    return acc


def kv_own_kernel(x0, x1, x2, pick, w, acc):
    for n, rows in enumerate((x0, x1, x2)):
        acc[n] = project(rows, pick, w, slice(0, 2 * W))


def kv_kernel(x0, x1, x2, pick, w, acc, gain, kv, kraw):
    for n, rows in enumerate((x0, x1, x2)):
        full = acc[n] + project(rows, pick, w, slice(0, 2 * W))
        if n == 0:
            kraw[...] = full[:, :W]
        for h in range(NH):
            kv[n, :, head(h)] = norm_rows(full[:, head(h)], gain[:, head(h)]).astype(BF16)
        kv[n, :, W:] = full[:, W:].astype(BF16)


def q_kernel(x, g, t, pick_o, pick_t, wo, wt, q_gain, k_gain, qraw, qn, d_att, tkv):
    q = project(x, pick_o, wo, slice(2 * W, 3 * W)) + project(x, pick_t, wt, slice(2 * W, 3 * W))
    qraw[...] = q
    for h in range(NH):
        qn[:, head(h)] = norm_rows(q[:, head(h)], q_gain[:, head(h)]).astype(BF16)
    last = slice(3 * W, 4 * W)
    d_att[...] = (project(g, pick_o, wo, last) + project(g, pick_t, wt, last)).astype(BF16)
    both = slice(0, 2 * W)
    s = project(t, pick_o, wo, both) + project(t, pick_t, wt, both)
    for h in range(NH):
        tkv[:, head(h)] = norm_rows(s[:, head(h)], k_gain[:, head(h)]).astype(BF16)
    tkv[:, W:] = s[:, W:].astype(BF16)


def attend_kernel(
    qn, d_att, qraw, q_gain, own, far, side, tkv, bias, att, dq, near_t, far_t, keys
):
    n = 4 * ROWS
    keys[:ROWS, :] = own[...]
    keys[ROWS : 2 * ROWS, :] = far[...]
    keys[2 * ROWS : n, :] = side[...]
    keys[n:, :] = tkv[...]
    for h in range(NH):
        qh = qn[:, head(h)]
        dh = d_att[:, head(h)]
        kh = keys[:, head(h)]
        vh = keys[:, val(h)]
        s = dot(qh, kh, NT) * SCALE + bias[...]
        e = jnp.exp(s - jnp.max(s, axis=-1, keepdims=True))
        p = e * (1.0 / jnp.sum(e, axis=-1, keepdims=True))
        pb = p.astype(BF16)
        att[:, head(h)] = dot(pb, vh).astype(BF16)
        dp = dot(dh, vh, NT)
        ds = (p * (dp - jnp.sum(p * dp, axis=-1, keepdims=True))).astype(BF16)
        d_q = dot(ds, kh) * SCALE
        dq[:, head(h)] = norm_pull(qraw[:, head(h)], q_gain[:, head(h)], d_q).astype(BF16)
        kt = (dot(ds[:, :n], qh, TN) * SCALE).astype(BF16)
        vt = dot(pb[:, :n], dh, TN).astype(BF16)
        near_t[:, head(h)] = kt[: 2 * ROWS]
        far_t[:, head(h)] = kt[2 * ROWS :]
        near_t[:, val(h)] = vt[: 2 * ROWS]
        far_t[:, val(h)] = vt[2 * ROWS :]


def out_kernel(att, dq, wo, wt, pick_o, pick_t, out, gq):
    for j in range(4):
        rows = slice(j * PART, (j + 1) * PART)
        o = dot(att[...], wo[rows, 3 * W :], NT).astype(BF16)
        t = dot(att[...], wt[rows, 3 * W :], NT).astype(BF16)
        out[j] = (dot(o, pick_o[...], NT) + dot(t, pick_t[...], NT)).astype(BF16)
        gq[0, j] = dot(dq[...], wo[rows, 2 * W : 3 * W], NT)
        gq[1, j] = dot(dq[...], wt[rows, 2 * W : 3 * W], NT)


def grad_kernel(own, in_a, in_b, kraw, k_gain, gq, wo, wt, pick_o, pick_t, o0, o1, o2, o3, out, res):
    total = own[...] + in_a[...].astype(F32) + in_b[...].astype(F32)
    parts = [
        norm_pull(kraw[:, head(h)], k_gain[:, head(h)], total[:, head(h)]).astype(BF16)
        for h in range(NH)
    ]
    d = jnp.concatenate(parts + [total[:, W:].astype(BF16)], axis=1)
    for j in range(4):
        rows = slice(j * PART, (j + 1) * PART)
        o = (gq[0, j] + dot(d, wo[rows, : 2 * W], NT)).astype(BF16)
        t = (gq[1, j] + dot(d, wt[rows, : 2 * W], NT)).astype(BF16)
        out[j] = (dot(o, pick_o[...], NT) + dot(t, pick_t[...], NT)).astype(BF16)
    res[...] = (
        o0[...].astype(F32) + o1[...].astype(F32) + o2[...].astype(F32) + o3[...].astype(F32)
    ).astype(BF16)


def to_heads(blocks, me):
    def block(to):
        return lax.dynamic_index_in_dim(blocks, to % 4, 0, keepdims=False)

    parts = [block(me)]
    for by in (1, 2, 3):
        pairs = [(i, (i + by) % 4) for i in range(4)]
        parts.append(lax.ppermute(block(me + by), "heads", pairs))
    return parts


def f32_sum(*terms):
    total = terms[0].astype(F32)
    for term in terms[1:]:
        total = total + term.astype(F32)
    return total


def per_device(
    x_tiles, x_text, w_query, w_key, w_value, w_output, q_gain, k_gain, text_mask, windows, grad_out
):
    place = lax.axis_index("seq")
    me = lax.axis_index("heads")
    core, x, col = place % 2, place // 32, place % 32
    beside = jnp.clip(jnp.where(core == 1, place + 1, place - 1), 0, 127)

    def far_even(who):
        row = lax.dynamic_index_in_dim(windows[:, 0], who, 0, keepdims=False)
        return (row == x) == (x % 2 == 0)

    mine_even, mate_even, beside_even = far_even(place), far_even(place ^ 1), far_even(beside)
    first_col = lax.dynamic_index_in_dim(windows[:, 1], place, 0, keepdims=False)
    use_core = (first_col == col) == (core == 0)
    q_gain = q_gain[None, :]
    k_gain = k_gain[None, :]

    at = jnp.arange(PART, dtype=jnp.int32)
    inner = at % BLOCK
    feature = lax.broadcasted_iota(jnp.int32, (W, PART), 0)

    def pick(which):
        natural = ((inner // 12 * 4 + at // BLOCK) * 2 + which) * 12 + inner % 12
        hit = (feature == natural[None, :]) & (inner < 48)[None, :]
        return hit.astype(BF16)

    pick_o, pick_t = pick(core), pick(1 - core)
    t = jnp.arange(TEXT, dtype=jnp.int32)
    token = place_of(t // 32 % 4, t // 2 % 4, t // 8 % 4, (t // 128) ^ core) * 2 + t % 2
    valid = jnp.sum(jnp.where(t[:, None] == token[None, :], text_mask[:, None], 0), axis=0)
    bias = jnp.concatenate(
        [jnp.zeros((4 * ROWS,), F32), jnp.where(valid == 1, 0.0, -1e30).astype(F32)]
    )[None, :]

    x_even, x_odd = row_even(x_tiles), row_odd(x_tiles)
    mine = jnp.concatenate([w_key, w_value, w_query, w_output], axis=1)
    four = over_zh(jnp.concatenate([mine, x_text], axis=0))
    block = jnp.concatenate([four[:, :12].reshape(48, 1536), four[:, 12:].reshape(8, 1536)], axis=0)
    wo = over_xy(block).reshape(16 * BLOCK, 1536)
    wt = core_mate(wo)
    texts = jnp.stack([wo, wt]).reshape(2, 16, BLOCK, 1536)[:, :, 48:].reshape(TEXT, 1536)

    acc = call(kv_own_kernel, shape((3, ROWS, 768), F32))(x_tiles, x_even, x_odd, pick_o, wo)
    kv, kraw = call(kv_kernel, (shape((3, ROWS, 768), BF16), shape((ROWS, W), F32)))(
        x_tiles, x_even, x_odd, pick_t, wt, acc, k_gain
    )
    own, even, odd = kv[0], kv[1], kv[2]
    from_mate = core_mate(jnp.concatenate([own, jnp.where(mate_even, even, odd)]))
    from_next = next_chip(jnp.concatenate([own, jnp.where(beside_even, even, odd)]))
    far = jnp.where(mine_even, even, odd)
    qraw, qn, d_att, tkv = call(
        q_kernel,
        (
            shape((ROWS, W), F32),
            shape((ROWS, W), BF16),
            shape((ROWS, W), BF16),
            shape((TEXT, 768), BF16),
        ),
    )(x_tiles, grad_out, texts, pick_o, pick_t, wo, wt, q_gain, k_gain)
    side = jnp.where(use_core, from_mate, from_next)
    att, dq, near_t, side_t = call(
        attend_kernel,
        (
            shape((ROWS, W), BF16),
            shape((ROWS, W), BF16),
            shape((2 * ROWS, 768), BF16),
            shape((2 * ROWS, 768), BF16),
        ),
        [pltpu.VMEM((1024, 768), BF16)],
    )(qn, d_att, qraw, q_gain, own, far, side, tkv, bias)

    zero = jnp.zeros_like(side_t)
    mate_t = core_mate(jnp.where(use_core, side_t, zero))
    next_t = next_chip(jnp.where(use_core, zero, side_t))
    out, gq = call(out_kernel, (shape((4, ROWS, W), BF16), shape((2, 4, ROWS, PART), F32)))(
        att, dq, wo, wt, pick_o, pick_t
    )
    outs = to_heads(out, me)
    zero = jnp.zeros((ROWS, 768), BF16)
    far_terms = (
        (mine_even, near_t[ROWS:]),
        (mate_even, mate_t[ROWS:]),
        (beside_even, next_t[ROWS:]),
    )
    to_even = f32_sum(*[jnp.where(flag, term, zero) for flag, term in far_terms]).astype(BF16)
    to_odd = f32_sum(*[jnp.where(flag, zero, term) for flag, term in far_terms]).astype(BF16)
    got_even, got_odd = row_even(to_even), row_odd(to_odd)
    own_t = f32_sum(near_t[:ROWS], mate_t[:ROWS], next_t[:ROWS])
    grad, out_tiles = call(
        grad_kernel, (shape((4, ROWS, W), BF16), shape((ROWS, W), BF16))
    )(own_t, got_even, got_odd, kraw, k_gain, gq, wo, wt, pick_o, pick_t, *outs)
    grad_tiles = f32_sum(*to_heads(grad, me)).astype(BF16)
    return (out_tiles, grad_tiles)


def solution(mesh):
    in_specs = (
        P("seq", None),
        P("seq", None),
        P("seq", "heads"),
        P("seq", "heads"),
        P("seq", "heads"),
        P("seq", "heads"),
        P("heads"),
        P("heads"),
        P(),
        P(),
        P("seq", None),
    )
    out_specs = (P("seq", "heads"), P("seq", "heads"))
    return jax.shard_map(
        per_device, mesh=mesh, in_specs=in_specs, out_specs=out_specs, check_vma=False
    )
```

```python
import functools

import jax
import jax.numpy as jnp
from jax import lax
from jax.experimental import pallas as pl
from jax.experimental.pallas import tpu as pltpu
from jax.sharding import PartitionSpec as P

HD = 128
NH = 3
W = NH * HD
ROWS = 192
TEXT = 256
EPS = 1e-6
SCALE = HD**-0.5
ZH_ORDER = (0, 1, 3, 2)
BLOCK = 56
PART = 4 * BLOCK
F32 = jnp.float32
BF16 = jnp.bfloat16
NT = (((1,), (1,)), ((), ()))
TN = (((0,), (0,)), ((), ()))


def place_of(x, zh, y, core):
    return ((x * 4 + zh) * 4 + y) * 2 + core


def all_places():
    return [(x, z, y, c) for x in range(4) for z in range(4) for y in range(4) for c in range(2)]


def seq_move(value, target):
    pairs = []
    for at in all_places():
        to = target(*at)
        if to is not None:
            pairs.append((place_of(*at), place_of(*to)))
    return lax.ppermute(value, "seq", pairs)


def core_mate(value):
    return seq_move(value, lambda x, z, y, c: (x, z, y, 1 - c))


def next_chip(value):
    def target(x, z, y, c):
        col = (z * 4 + y) * 2 + c
        col = col + 1 if c == 1 else col - 1
        if not 0 <= col < 32:
            return None
        return (x, col // 8, col // 2 % 4, col % 2)

    return seq_move(value, target)


def row_even(value):
    return seq_move(value, lambda x, z, y, c: (x ^ 1, z, y, c))


def row_odd(value):
    return seq_move(value, lambda x, z, y, c: (3 - x, z, y, c) if x in (1, 2) else None)


def give_all(value, groups):
    copies = jnp.broadcast_to(value[None], (len(groups[0]),) + value.shape)
    return lax.all_to_all(copies, "seq", 0, 0, axis_index_groups=groups)


def across_zh(value, mask):
    return seq_move(value, lambda x, z, y, c: (x, z ^ mask, y, c))


def over_xy(value):
    four = range(4)
    return give_all(
        value,
        [[place_of(x, z, y, c) for x in four for y in four] for z in four for c in range(2)],
    )


def dot(a, b, dims=(((1,), (0,)), ((), ()))):
    return lax.dot_general(a, b, dims, preferred_element_type=F32)


def norm_rows(a, gain):
    r = lax.rsqrt(jnp.mean(a * a, axis=-1, keepdims=True) + EPS)
    return a * r * gain


def norm_pull(a, gain, dy):
    r = lax.rsqrt(jnp.mean(a * a, axis=-1, keepdims=True) + EPS)
    t = dy * gain
    return r * t - a * (r * r * r * jnp.mean(t * a, axis=-1, keepdims=True))


def head(h):
    return slice(h * HD, (h + 1) * HD)


def val(h):
    return slice(W + h * HD, W + (h + 1) * HD)


def call(kernel, outs, scratch=(), mib=32, flops=10**9, flagged=False, count=0):
    spaces = [pltpu.SMEM if flagged and n == 0 else pltpu.VMEM for n in range(count)]
    return pl.pallas_call(
        kernel,
        out_shape=outs,
        in_specs=[pl.BlockSpec(memory_space=space) for space in spaces],
        scratch_shapes=scratch,
        compiler_params=pltpu.CompilerParams(vmem_limit_bytes=mib * 2**20),
        cost_estimate=pl.CostEstimate(flops=flops, bytes_accessed=8 * 10**6, transcendentals=0),
    )


def shape(dims, dtype):
    return jax.ShapeDtypeStruct(dims, dtype)


def project(rows, pick, w, cols):
    acc = None
    for j in range(4):
        xs = dot(rows[:, j * W : (j + 1) * W], pick[...]).astype(BF16)
        term = dot(xs, w[j * PART : (j + 1) * PART, cols])
        acc = term if acc is None else acc + term
    return acc


def project_parts(flags, parts, pick, w):
    acc = None
    for n, part in enumerate(parts):
        at = pl.multiple_of(flags[2 + n] * PART, PART)
        xs = dot(part[...], pick[...]).astype(BF16)
        term = dot(xs, w[pl.ds(at, PART), : 2 * W])
        acc = term if acc is None else acc + term
    return acc


KVQ = slice(0, 3 * W)
KV = slice(0, 2 * W)
LAST = slice(3 * W, 4 * W)


def first_kernel(flags, x, g, p0, p1, p2, p3, pick, w, acc_x, acc_g, acc_p):
    acc_x[...] = project(x, pick, w, KVQ)
    acc_g[...] = project(g, pick, w, LAST)
    acc_p[...] = project_parts(flags, (p0, p1, p2, p3), pick, w)


def attend_kernel(
    flags,
    x,
    g,
    p0,
    p1,
    p2,
    p3,
    text,
    pick_o,
    pick_t,
    wo,
    wt,
    acc_x,
    acc_g,
    acc_p,
    q_gain,
    k_gain,
    bias,
    att,
    dq,
    near_t,
    even_t,
    odd_t,
    kraw,
    keys,
):
    n = 4 * ROWS
    mine = acc_x[...] + project(x, pick_t, wt, KVQ)
    d_att = (acc_g[...] + project(g, pick_t, wt, LAST)).astype(BF16)
    others = acc_p[...] + project_parts(flags, (p0, p1, p2, p3), pick_t, wt)
    words = project(text, pick_o, wo, KV) + project(text, pick_t, wt, KV)
    kraw[...] = mine[:, :W]
    for low, high, values in ((0, ROWS, mine), (ROWS, n, others), (n, n + TEXT, words)):
        for h in range(NH):
            kn = norm_rows(values[:, head(h)], k_gain[:, head(h)])
            keys[low:high, head(h)] = kn.astype(BF16)
        keys[low:high, W:] = values[:, W : 2 * W].astype(BF16)
    even = flags[0].astype(F32)
    odd = 1.0 - even
    for h in range(NH):
        q = mine[:, val(NH + h)]
        qh = norm_rows(q, q_gain[:, head(h)]).astype(BF16)
        dh = d_att[:, head(h)]
        kh = keys[:, head(h)]
        vh = keys[:, val(h)]
        s = dot(qh, kh, NT) * SCALE + bias[...]
        e = jnp.exp(s - jnp.max(s, axis=-1, keepdims=True))
        p = e * (1.0 / jnp.sum(e, axis=-1, keepdims=True))
        pb = p.astype(BF16)
        att[:, head(h)] = dot(pb, vh).astype(BF16)
        dp = dot(dh, vh, NT)
        ds = (p * (dp - jnp.sum(p * dp, axis=-1, keepdims=True))).astype(BF16)
        d_q = dot(ds, kh) * SCALE
        dq[:, head(h)] = norm_pull(q, q_gain[:, head(h)], d_q).astype(BF16)
        kt = dot(ds[:, :n], qh, TN) * SCALE
        vt = dot(pb[:, :n], dh, TN)
        for lanes, term in ((head(h), kt), (val(h), vt)):
            near_t[:, lanes] = term[: 2 * ROWS].astype(BF16)
            even_t[:, lanes] = (term[2 * ROWS :] * even).astype(BF16)
            odd_t[:, lanes] = (term[2 * ROWS :] * odd).astype(BF16)


def out_kernel(att, dq, wo, wt, pick_o, pick_t, out, gq):
    for j in range(4):
        rows = slice(j * PART, (j + 1) * PART)
        o = dot(att[...], wo[rows, 3 * W :], NT).astype(BF16)
        t = dot(att[...], wt[rows, 3 * W :], NT).astype(BF16)
        out[j] = (dot(o, pick_o[...], NT) + dot(t, pick_t[...], NT)).astype(BF16)
        gq[0, j] = dot(dq[...], wo[rows, 2 * W : 3 * W], NT)
        gq[1, j] = dot(dq[...], wt[rows, 2 * W : 3 * W], NT)


def grad_kernel(own, in_a, in_b, kraw, k_gain, gq, wo, wt, pick_o, pick_t, o0, o1, o2, o3, out, res):
    total = own[...] + in_a[...].astype(F32) + in_b[...].astype(F32)
    parts = [
        norm_pull(kraw[:, head(h)], k_gain[:, head(h)], total[:, head(h)]).astype(BF16)
        for h in range(NH)
    ]
    d = jnp.concatenate(parts + [total[:, W:].astype(BF16)], axis=1)
    for j in range(4):
        rows = slice(j * PART, (j + 1) * PART)
        o = (gq[0, j] + dot(d, wo[rows, : 2 * W], NT)).astype(BF16)
        t = (gq[1, j] + dot(d, wt[rows, : 2 * W], NT)).astype(BF16)
        out[j] = (dot(o, pick_o[...], NT) + dot(t, pick_t[...], NT)).astype(BF16)
    res[...] = (
        o0[...].astype(F32) + o1[...].astype(F32) + o2[...].astype(F32) + o3[...].astype(F32)
    ).astype(BF16)


def to_heads(blocks, me):
    def block(to):
        return lax.dynamic_index_in_dim(blocks, to % 4, 0, keepdims=False)

    return [block(me)] + [head_shift(block(me + by), by) for by in (1, 2, 3)]


def f32_sum(*terms):
    total = terms[0].astype(F32)
    for term in terms[1:]:
        total = total + term.astype(F32)
    return total


def head_shift(value, by):
    return lax.ppermute(value, "heads", [(i, (i + by) % 4) for i in range(4)])


def per_device(
    x_tiles, x_text, w_query, w_key, w_value, w_output, q_gain, k_gain, text_mask, windows, grad_out
):
    place = lax.axis_index("seq")
    me = lax.axis_index("heads")
    core, zh, x, col = place % 2, place // 8 % 4, place // 32, place % 32
    window = lax.dynamic_slice(windows, (place, jnp.int32(0)), (1, 2))
    use_even = (window[0, 0] == x) == (x % 2 == 0)
    use_core = (window[0, 1] == col) == (core == 0)
    q_gain = q_gain[None, :]
    k_gain = k_gain[None, :]
    blocks = [(me - by) % 4 for by in range(4)]
    flags = jnp.stack([use_even.astype(jnp.int32), use_core.astype(jnp.int32)] + blocks)

    mine = jnp.concatenate([w_key, w_value, w_query, w_output], axis=1)
    mine = jnp.concatenate([mine, x_text], axis=0)
    quarter = lax.dynamic_slice(x_tiles, (jnp.int32(0), me * W), (ROWS, W))
    two = jnp.stack([mine, across_zh(mine, 1)])
    side = jnp.where(use_core, core_mate(quarter), next_chip(quarter))
    four = jnp.concatenate([two, across_zh(two, 3)])
    pair = jnp.concatenate([quarter, side])
    far = jnp.where(use_even, row_even(pair), row_odd(pair))
    others = jnp.concatenate([side, far])
    block = jnp.concatenate([four[:, :12].reshape(48, 1536), four[:, 12:].reshape(8, 1536)], axis=0)
    block, others = lax.optimization_barrier((block, others))
    parts = [others] + [head_shift(others, by) for by in (1, 2, 3)]
    wo = over_xy(block).reshape(16 * BLOCK, 1536)
    wo, *parts = lax.optimization_barrier((wo, *parts))
    wt = core_mate(wo)

    at = jnp.arange(PART, dtype=jnp.int32)
    inner = at % BLOCK
    feature = lax.broadcasted_iota(jnp.int32, (W, PART), 0)
    z_order = jnp.array(ZH_ORDER, jnp.int32)

    def pick(which):
        natural = (((z_order[inner // 12 % 4] ^ zh) * 4 + at // BLOCK) * 2 + which) * 12 + inner % 12
        hit = (feature == natural[None, :]) & (inner < 48)[None, :]
        return hit.astype(BF16)

    pick_o, pick_t = pick(core), pick(1 - core)
    t = jnp.arange(TEXT, dtype=jnp.int32)
    token = place_of(t // 32 % 4, z_order[t // 2 % 4] ^ zh, t // 8 % 4, (t // 128) ^ core) * 2 + t % 2
    valid = jnp.sum(jnp.where(t[:, None] == token[None, :], text_mask[:, None], 0), axis=0)
    bias = jnp.concatenate(
        [jnp.zeros((4 * ROWS,), F32), jnp.where(valid == 1, 0.0, -1e30).astype(F32)]
    )[None, :]

    accs = call(
        first_kernel,
        (shape((ROWS, 3 * W), F32), shape((ROWS, W), F32), shape((3 * ROWS, 2 * W), F32)),
        flagged=True,
        count=9,
    )(flags, x_tiles, grad_out, *parts, pick_o, wo)
    texts = jnp.stack([wo, wt]).reshape(2, 16, BLOCK, 1536)[:, :, 48:].reshape(TEXT, 1536)
    att, dq, near_t, even_t, odd_t, kraw = call(
        attend_kernel,
        (
            shape((ROWS, W), BF16),
            shape((ROWS, W), BF16),
            shape((2 * ROWS, 768), BF16),
            shape((2 * ROWS, 768), BF16),
            shape((2 * ROWS, 768), BF16),
            shape((ROWS, W), F32),
        ),
        [pltpu.VMEM((1024, 768), BF16)],
        mib=40,
        flagged=True,
        count=18,
    )(flags, x_tiles, grad_out, *parts, texts, pick_o, pick_t, wo, wt, *accs, q_gain, k_gain, bias)

    got_even, got_odd = row_even(even_t), row_odd(odd_t)
    out, gq = call(
        out_kernel, (shape((4, ROWS, W), BF16), shape((2, 4, ROWS, PART), F32)), count=6
    )(att, dq, wo, wt, pick_o, pick_t)
    outs = to_heads(out, me)
    own_t = f32_sum(near_t[:ROWS], got_even[:ROWS], got_odd[:ROWS])
    side_t = f32_sum(near_t[ROWS:], got_even[ROWS:], got_odd[ROWS:]).astype(BF16)
    zero = jnp.zeros((ROWS, 768), BF16)
    mate_t = core_mate(jnp.where(use_core, side_t, zero))
    next_t = next_chip(jnp.where(use_core, zero, side_t))
    grad, out_tiles = call(
        grad_kernel, (shape((4, ROWS, W), BF16), shape((ROWS, W), BF16)), count=14
    )(own_t, mate_t, next_t, kraw, k_gain, gq, wo, wt, pick_o, pick_t, *outs)
    grad_tiles = f32_sum(*to_heads(grad, me)).astype(BF16)
    return (out_tiles, grad_tiles)


def solution(mesh):
    in_specs = (
        P("seq", None),
        P("seq", None),
        P("seq", "heads"),
        P("seq", "heads"),
        P("seq", "heads"),
        P("seq", "heads"),
        P("heads"),
        P("heads"),
        P(),
        P(),
        P("seq", None),
    )
    out_specs = (P("seq", "heads"), P("seq", "heads"))
    return jax.shard_map(
        per_device, mesh=mesh, in_specs=in_specs, out_specs=out_specs, check_vma=False
    )
```

```python
import functools

import jax
import jax.numpy as jnp
from jax import lax
from jax.experimental import pallas as pl
from jax.experimental.pallas import tpu as pltpu
from jax.sharding import PartitionSpec as P

HD = 128
NH = 3
W = NH * HD
ROWS = 192
TEXT = 256
EPS = 1e-6
SCALE = HD**-0.5
OUT_COST = 10**9
GRAD_COST = 10**9
BLOCK = 56
PART = 4 * BLOCK
F32 = jnp.float32
BF16 = jnp.bfloat16
NT = (((1,), (1,)), ((), ()))
TN = (((0,), (0,)), ((), ()))


def place_of(x, zh, y, core):
    return ((x * 4 + zh) * 4 + y) * 2 + core


def all_places():
    return [(x, z, y, c) for x in range(4) for z in range(4) for y in range(4) for c in range(2)]


def seq_move(value, target):
    pairs = []
    for at in all_places():
        to = target(*at)
        if to is not None:
            pairs.append((place_of(*at), place_of(*to)))
    return lax.ppermute(value, "seq", pairs)


def core_mate(value):
    return seq_move(value, lambda x, z, y, c: (x, z, y, 1 - c))


def next_chip(value):
    def target(x, z, y, c):
        col = (z * 4 + y) * 2 + c
        col = col + 1 if c == 1 else col - 1
        if not 0 <= col < 32:
            return None
        return (x, col // 8, col // 2 % 4, col % 2)

    return seq_move(value, target)


def row_even(value):
    return seq_move(value, lambda x, z, y, c: (x ^ 1, z, y, c))


def row_odd(value):
    return seq_move(value, lambda x, z, y, c: (3 - x, z, y, c) if x in (1, 2) else None)


def give_all(value, groups):
    copies = jnp.broadcast_to(value[None], (len(groups[0]),) + value.shape)
    return lax.all_to_all(copies, "seq", 0, 0, axis_index_groups=groups)


def over_zh(value):
    four = range(4)
    return give_all(
        value,
        [[place_of(x, z, y, c) for z in four] for x in four for y in four for c in range(2)],
    )


def over_xy(value):
    four = range(4)
    return give_all(
        value,
        [[place_of(x, z, y, c) for x in four for y in four] for z in four for c in range(2)],
    )


def dot(a, b, dims=(((1,), (0,)), ((), ()))):
    return lax.dot_general(a, b, dims, preferred_element_type=F32)


def norm_rows(a, gain):
    r = lax.rsqrt(jnp.mean(a * a, axis=-1, keepdims=True) + EPS)
    return a * r * gain


def norm_pull(a, gain, dy):
    r = lax.rsqrt(jnp.mean(a * a, axis=-1, keepdims=True) + EPS)
    t = dy * gain
    return r * t - a * (r * r * r * jnp.mean(t * a, axis=-1, keepdims=True))


def head(h):
    return slice(h * HD, (h + 1) * HD)


def val(h):
    return slice(W + h * HD, W + (h + 1) * HD)


def call(kernel, outs, spaces, scratch=(), mib=16, flops=10**9):
    place = {"s": pltpu.SMEM, "h": pltpu.HBM, "v": pltpu.VMEM}
    return pl.pallas_call(
        kernel,
        out_shape=outs,
        in_specs=[pl.BlockSpec(memory_space=place[space]) for space in spaces],
        scratch_shapes=scratch,
        compiler_params=pltpu.CompilerParams(vmem_limit_bytes=mib * 2**20),
        cost_estimate=pl.CostEstimate(flops=flops, bytes_accessed=8 * 10**6, transcendentals=0),
    )


def shape(dims, dtype):
    return jax.ShapeDtypeStruct(dims, dtype)


KVQ = slice(0, 3 * W)
KV = slice(0, 2 * W)
LAST = slice(3 * W, 4 * W)
HALF_TEXT = TEXT // 2


def pick_rows(rows, pick, out):
    for j in range(4):
        out[j] = dot(rows[:, j * W : (j + 1) * W], pick[...]).astype(BF16)


def pick_kernel(*refs):
    n = (len(refs) - 2) // 3
    pick_o, pick_t = refs[n], refs[n + 1]
    for i in range(n):
        pick_rows(refs[i], pick_o, refs[n + 2 + 2 * i])
        pick_rows(refs[i], pick_t, refs[n + 3 + 2 * i])


def pick_parts_kernel(p0, p1, p2, p3, pick_o, pick_t, out_o, out_t):
    for n, part in enumerate((p0, p1, p2, p3)):
        out_o[n] = dot(part[...], pick_o[...]).astype(BF16)
        out_t[n] = dot(part[...], pick_t[...]).astype(BF16)


def project(picked, w, cols, order=(0, 1, 2, 3)):
    acc = None
    for n, j in enumerate(order):
        if isinstance(j, int):
            rows = w[j * PART : (j + 1) * PART, cols]
        else:
            rows = w[pl.ds(pl.multiple_of(j * PART, PART), PART), cols]
        term = dot(picked[n], rows)
        acc = term if acc is None else acc + term
    return acc


def picked_value(rows, pick):
    return [dot(rows[:, j * W : (j + 1) * W], pick[...]).astype(BF16) for j in range(4)]


def part_order(flags):
    return [flags[2 + n] for n in range(4)]


def first_kernel(
    flags, x, g, f, p, pick_o, pick_t, lines, w, acc_x, acc_g, acc_f, acc_p, acc_t, text
):
    acc_x[...] = project(x, w, KVQ)
    acc_g[...] = project(g, w, LAST)
    acc_f[...] = project(f, w, KV)
    acc_p[...] = project(p, w, KV, part_order(flags))
    t = dot(lines[...], w[...]).astype(BF16)
    acc_t[...] = project(picked_value(t, pick_o), w, KV)
    pick_rows(t, pick_t, text)


def attend_kernel(
    flags,
    x,
    g,
    f,
    p,
    text,
    pick_o,
    pick_t,
    lines,
    wo,
    wt,
    acc_x,
    acc_g,
    acc_f,
    acc_p,
    acc_t,
    q_gain,
    k_gain,
    bias,
    att,
    dq,
    near_t,
    even_t,
    odd_t,
    kraw,
    keys,
):
    n = 4 * ROWS
    mine = acc_x[...] + project(x, wt, KVQ)
    d_att = (acc_g[...] + project(g, wt, LAST)).astype(BF16)
    behind = acc_f[...] + project(f, wt, KV)
    beside = acc_p[...] + project(p, wt, KV, part_order(flags))
    words = acc_t[...] + project(text, wt, KV)
    t = dot(lines[...], wt[...]).astype(BF16)
    more = project(picked_value(t, pick_o), wo, KV) + project(picked_value(t, pick_t), wt, KV)
    kraw[...] = mine[:, :W]
    low = 0
    for values in (mine, beside[:ROWS], behind, beside[ROWS:], words, more):
        high = low + values.shape[0]
        for h in range(NH):
            kn = norm_rows(values[:, head(h)], k_gain[:, head(h)])
            keys[low:high, head(h)] = kn.astype(BF16)
        keys[low:high, W:] = values[:, W : 2 * W].astype(BF16)
        low = high
    even = flags[0].astype(F32)
    odd = 1.0 - even
    for h in range(NH):
        q = mine[:, val(NH + h)]
        qh = norm_rows(q, q_gain[:, head(h)]).astype(BF16)
        dh = d_att[:, head(h)]
        kh = keys[:, head(h)]
        vh = keys[:, val(h)]
        s = dot(qh, kh, NT) * SCALE + bias[...]
        e = jnp.exp(s - jnp.max(s, axis=-1, keepdims=True))
        p_h = e * (1.0 / jnp.sum(e, axis=-1, keepdims=True))
        pb = p_h.astype(BF16)
        att[:, head(h)] = dot(pb, vh).astype(BF16)
        dp = dot(dh, vh, NT)
        ds = (p_h * (dp - jnp.sum(p_h * dp, axis=-1, keepdims=True))).astype(BF16)
        d_q = dot(ds, kh) * SCALE
        dq[:, head(h)] = norm_pull(q, q_gain[:, head(h)], d_q).astype(BF16)
        kt = dot(ds[:, :n], qh, TN) * SCALE
        vt = dot(pb[:, :n], dh, TN)
        for lanes, term in ((head(h), kt), (val(h), vt)):
            near_t[:, lanes] = term[: 2 * ROWS].astype(BF16)
            even_t[:, lanes] = (term[2 * ROWS :] * even).astype(BF16)
            odd_t[:, lanes] = (term[2 * ROWS :] * odd).astype(BF16)


def out_kernel(att, dq, wo, wt, pick_o, pick_t, out, gq):
    for j in range(4):
        rows = slice(j * PART, (j + 1) * PART)
        o = dot(att[...], wo[rows, 3 * W :], NT).astype(BF16)
        t = dot(att[...], wt[rows, 3 * W :], NT).astype(BF16)
        out[j] = (dot(o, pick_o[...], NT) + dot(t, pick_t[...], NT)).astype(BF16)
        gq[0, j] = dot(dq[...], wo[rows, 2 * W : 3 * W], NT)
        gq[1, j] = dot(dq[...], wt[rows, 2 * W : 3 * W], NT)


def term_kernel(flags, near_t, got_even, got_odd, own, to_mate, to_next):
    total = near_t[...].astype(F32) + got_even[...].astype(F32) + got_odd[...].astype(F32)
    own[...] = total[:ROWS]
    mate = flags[1].astype(F32)
    to_mate[...] = (total[ROWS:] * mate).astype(BF16)
    to_next[...] = (total[ROWS:] * (1.0 - mate)).astype(BF16)


def grad_kernel(own, in_a, in_b, kraw, k_gain, gq, wo, wt, pick_o, pick_t, o0, o1, o2, o3, out, res):
    total = own[...] + in_a[...].astype(F32) + in_b[...].astype(F32)
    parts = [
        norm_pull(kraw[:, head(h)], k_gain[:, head(h)], total[:, head(h)]).astype(BF16)
        for h in range(NH)
    ]
    d = jnp.concatenate(parts + [total[:, W:].astype(BF16)], axis=1)
    for j in range(4):
        rows = slice(j * PART, (j + 1) * PART)
        o = (gq[0, j] + dot(d, wo[rows, : 2 * W], NT)).astype(BF16)
        t = (gq[1, j] + dot(d, wt[rows, : 2 * W], NT)).astype(BF16)
        out[j] = (dot(o, pick_o[...], NT) + dot(t, pick_t[...], NT)).astype(BF16)
    res[...] = f32_sum(o0[...], o1[...], o2[...], o3[...]).astype(BF16)


def to_heads(blocks, me):
    def block(to):
        return lax.dynamic_index_in_dim(blocks, to & 3, 0, keepdims=False)

    return [block(me)] + [head_shift(block(me + by), by) for by in (1, 2, 3)]


def f32_sum(*terms):
    total = terms[0].astype(F32)
    for term in terms[1:]:
        total = total + term.astype(F32)
    return total


def head_shift(value, by):
    return lax.ppermute(value, "heads", [(i, (i + by) % 4) for i in range(4)])


def per_device(
    x_tiles, x_text, w_query, w_key, w_value, w_output, q_gain, k_gain, text_mask, windows, grad_out
):
    place = lax.axis_index("seq")
    me = lax.axis_index("heads")
    core, x, col = place & 1, place >> 5, place & 31
    window = lax.dynamic_slice(windows, (place, jnp.int32(0)), (1, 2))
    use_even = (window[0, 0] == x) == ((x & 1) == 0)
    use_core = (window[0, 1] == col) == (core == 0)
    q_gain = q_gain[None, :]
    k_gain = k_gain[None, :]
    blocks = [(me - by) & 3 for by in range(4)]
    flags = jnp.stack([use_even.astype(jnp.int32), use_core.astype(jnp.int32)] + blocks)

    at = jnp.arange(PART, dtype=jnp.int32)
    inner = at % BLOCK
    feature = lax.broadcasted_iota(jnp.int32, (W, PART), 0)

    def pick(which):
        natural = ((inner // 12 * 4 + at // BLOCK) * 2 + which) * 12 + inner % 12
        hit = (feature == natural[None, :]) & (inner < 48)[None, :]
        return hit.astype(BF16)

    pick_o, pick_t = pick(core), pick(1 - core)
    t = jnp.arange(HALF_TEXT, dtype=jnp.int32)
    line = t // 8 * BLOCK + 48 + t % 8
    lines = (line[:, None] == jnp.arange(16 * BLOCK, dtype=jnp.int32)[None, :]).astype(BF16)
    t = jnp.arange(TEXT, dtype=jnp.int32)
    token = place_of(t // 32 % 4, t // 2 % 4, t // 8 % 4, (t // 128) ^ core) * 2 + t % 2
    valid = jnp.sum(jnp.where(t[:, None] == token[None, :], text_mask[:, None], 0), axis=0)
    bias = jnp.concatenate(
        [jnp.zeros((4 * ROWS,), F32), jnp.where(valid == 1, 0.0, -1e30).astype(F32)]
    )[None, :]

    quarter = lax.dynamic_slice(x_tiles, (jnp.int32(0), me * W), (ROWS, W))
    mine = jnp.concatenate([w_key, w_value, w_query, w_output], axis=1)
    four = over_zh(jnp.concatenate([mine, x_text], axis=0))
    behind = jnp.where(use_even, row_even(x_tiles), row_odd(x_tiles))
    side = jnp.where(use_core, core_mate(quarter), next_chip(quarter))
    side, behind, pick_o, pick_t, flags = lax.optimization_barrier(
        (side, behind, pick_o, pick_t, flags)
    )
    corner = jnp.where(use_even, row_even(side), row_odd(side))
    beside = jnp.concatenate([side, corner])
    block = jnp.concatenate([four[:, :12].reshape(48, 1536), four[:, 12:].reshape(8, 1536)], axis=0)
    block, beside, lines, bias = lax.optimization_barrier((block, beside, lines, bias))
    parts = [beside] + [head_shift(beside, by) for by in (1, 2, 3)]
    wo = over_xy(block).reshape(16 * BLOCK, 1536)
    picked = shape((4, ROWS, PART), BF16)
    x_o, x_t, g_o, g_t, f_o, f_t = call(pick_kernel, (picked,) * 6, "v" * 5)(
        x_tiles, grad_out, behind, pick_o, pick_t
    )
    p_o, p_t = call(pick_parts_kernel, (shape((4, 2 * ROWS, PART), BF16),) * 2, "v" * 6)(
        *parts, pick_o, pick_t
    )
    wo, x_o, x_t, g_o, g_t, f_o, f_t, p_o, p_t = lax.optimization_barrier(
        (wo, x_o, x_t, g_o, g_t, f_o, f_t, p_o, p_t)
    )
    wt = core_mate(wo)

    *accs, text = call(
        first_kernel,
        (
            shape((ROWS, 3 * W), F32),
            shape((ROWS, W), F32),
            shape((ROWS, 2 * W), F32),
            shape((2 * ROWS, 2 * W), F32),
            shape((HALF_TEXT, 2 * W), F32),
            shape((4, HALF_TEXT, PART), BF16),
        ),
        "s" + "v" * 8,
    )(flags, x_o, g_o, f_o, p_o, pick_o, pick_t, lines, wo)
    att, dq, near_t, even_t, odd_t, kraw = call(
        attend_kernel,
        (
            shape((ROWS, W), BF16),
            shape((ROWS, W), BF16),
            shape((2 * ROWS, 768), BF16),
            shape((2 * ROWS, 768), BF16),
            shape((2 * ROWS, 768), BF16),
            shape((ROWS, W), F32),
        ),
        "s" + "v" * 18,
        scratch=[pltpu.VMEM((1024, 768), BF16)],
        mib=28,
    )(flags, x_t, g_t, f_t, p_t, text, pick_o, pick_t, lines, wo, wt, *accs, q_gain, k_gain, bias)

    got_even, got_odd = row_even(even_t), row_odd(odd_t)
    out, gq = call(
        out_kernel,
        (shape((4, ROWS, W), BF16), shape((2, 4, ROWS, PART), F32)),
        "v" * 6,
        flops=OUT_COST,
    )(att, dq, wo, wt, pick_o, pick_t)
    outs = to_heads(out, me)
    got_even, got_odd, outs[1], outs[2] = lax.optimization_barrier(
        (got_even, got_odd, outs[1], outs[2])
    )
    own_t, to_mate, to_next = call(
        term_kernel,
        (shape((ROWS, 768), F32), shape((ROWS, 768), BF16), shape((ROWS, 768), BF16)),
        "svvv",
        mib=8,
    )(flags, near_t, got_even, got_odd)
    mate_t, next_t = core_mate(to_mate), next_chip(to_next)
    grad, out_tiles = call(
        grad_kernel,
        (shape((4, ROWS, W), BF16), shape((ROWS, W), BF16)),
        "v" * 14,
        flops=GRAD_COST,
    )(own_t, mate_t, next_t, kraw, k_gain, gq, wo, wt, pick_o, pick_t, *outs)
    grads = lax.all_to_all(grad, "heads", 0, 0)
    return (out_tiles, f32_sum(*[grads[n] for n in range(4)]).astype(BF16))


def solution(mesh):
    in_specs = (
        P("seq", None),
        P("seq", None),
        P("seq", "heads"),
        P("seq", "heads"),
        P("seq", "heads"),
        P("seq", "heads"),
        P("heads"),
        P("heads"),
        P(),
        P(),
        P("seq", None),
    )
    out_specs = (P("seq", "heads"), P("seq", "heads"))
    return jax.shard_map(
        per_device, mesh=mesh, in_specs=in_specs, out_specs=out_specs, check_vma=False
    )
```

```python
import functools

import jax
import jax.numpy as jnp
from jax import lax
from jax.experimental import pallas as pl
from jax.experimental.pallas import tpu as pltpu
from jax.sharding import PartitionSpec as P

HD = 128
NH = 3
W = NH * HD
ROWS = 192
TEXT = 256
EPS = 1e-6
SCALE = HD**-0.5
OUT_COST = 10**9
TERM_COST = 10**11
GRAD_COST = 10**9
BLOCK = 56
PART = 4 * BLOCK
F32 = jnp.float32
BF16 = jnp.bfloat16
NT = (((1,), (1,)), ((), ()))
TN = (((0,), (0,)), ((), ()))


def place_of(x, zh, y, core):
    return ((x * 4 + zh) * 4 + y) * 2 + core


def all_places():
    return [(x, z, y, c) for x in range(4) for z in range(4) for y in range(4) for c in range(2)]


def seq_move(value, target):
    pairs = []
    for at in all_places():
        to = target(*at)
        if to is not None:
            pairs.append((place_of(*at), place_of(*to)))
    return lax.ppermute(value, "seq", pairs)


def core_mate(value):
    return seq_move(value, lambda x, z, y, c: (x, z, y, 1 - c))


def next_chip(value):
    def target(x, z, y, c):
        col = (z * 4 + y) * 2 + c
        col = col + 1 if c == 1 else col - 1
        if not 0 <= col < 32:
            return None
        return (x, col // 8, col // 2 % 4, col % 2)

    return seq_move(value, target)


def row_even(value):
    return seq_move(value, lambda x, z, y, c: (x ^ 1, z, y, c))


def row_odd(value):
    return seq_move(value, lambda x, z, y, c: (3 - x, z, y, c) if x in (1, 2) else None)


def give_all(value, groups):
    copies = jnp.broadcast_to(value[None], (len(groups[0]),) + value.shape)
    return lax.all_to_all(copies, "seq", 0, 0, axis_index_groups=groups)


def over_zh(value):
    four = range(4)
    return give_all(
        value,
        [[place_of(x, z, y, c) for z in four] for x in four for y in four for c in range(2)],
    )


def over_xy(value):
    four = range(4)
    return give_all(
        value,
        [[place_of(x, z, y, c) for x in four for y in four] for z in four for c in range(2)],
    )


def dot(a, b, dims=(((1,), (0,)), ((), ()))):
    return lax.dot_general(a, b, dims, preferred_element_type=F32)


def norm_rows(a, gain):
    r = lax.rsqrt(jnp.mean(a * a, axis=-1, keepdims=True) + EPS)
    return a * r * gain


def norm_pull(a, gain, dy):
    r = lax.rsqrt(jnp.mean(a * a, axis=-1, keepdims=True) + EPS)
    t = dy * gain
    return r * t - a * (r * r * r * jnp.mean(t * a, axis=-1, keepdims=True))


def head(h):
    return slice(h * HD, (h + 1) * HD)


def val(h):
    return slice(W + h * HD, W + (h + 1) * HD)


def call(kernel, outs, spaces, scratch=(), mib=16, flops=10**9):
    place = {"s": pltpu.SMEM, "h": pltpu.HBM, "v": pltpu.VMEM}
    return pl.pallas_call(
        kernel,
        out_shape=outs,
        in_specs=[pl.BlockSpec(memory_space=place[space]) for space in spaces],
        scratch_shapes=scratch,
        compiler_params=pltpu.CompilerParams(vmem_limit_bytes=mib * 2**20),
        cost_estimate=pl.CostEstimate(flops=flops, bytes_accessed=8 * 10**6, transcendentals=0),
    )


def shape(dims, dtype):
    return jax.ShapeDtypeStruct(dims, dtype)


KVQ = slice(0, 3 * W)
KV = slice(0, 2 * W)
LAST = slice(3 * W, 4 * W)
HALF_TEXT = TEXT // 2


def pick_rows(rows, pick, out):
    for j in range(4):
        out[j] = dot(rows[:, j * W : (j + 1) * W], pick[...]).astype(BF16)


def pick_kernel(*refs):
    n = (len(refs) - 2) // 3
    pick_o, pick_t = refs[n], refs[n + 1]
    for i in range(n):
        pick_rows(refs[i], pick_o, refs[n + 2 + 2 * i])
        pick_rows(refs[i], pick_t, refs[n + 3 + 2 * i])


def pick_parts_kernel(p0, p1, p2, p3, pick_o, pick_t, out_o, out_t):
    for n, part in enumerate((p0, p1, p2, p3)):
        out_o[n] = dot(part[...], pick_o[...]).astype(BF16)
        out_t[n] = dot(part[...], pick_t[...]).astype(BF16)


def project(picked, w, cols, order=(0, 1, 2, 3)):
    acc = None
    for n, j in enumerate(order):
        if isinstance(j, int):
            rows = w[j * PART : (j + 1) * PART, cols]
        else:
            rows = w[pl.ds(pl.multiple_of(j * PART, PART), PART), cols]
        term = dot(picked[n], rows)
        acc = term if acc is None else acc + term
    return acc


def picked_value(rows, pick):
    return [dot(rows[:, j * W : (j + 1) * W], pick[...]).astype(BF16) for j in range(4)]


def part_order(flags):
    return [flags[2 + n] for n in range(4)]


def first_kernel(
    flags, x, g, f, p, pick_o, pick_t, lines, w, acc_x, acc_g, acc_f, acc_p, acc_t, text
):
    acc_x[...] = project(x, w, KVQ)
    acc_g[...] = project(g, w, LAST)
    acc_f[...] = project(f, w, KV)
    acc_p[...] = project(p, w, KV, part_order(flags))
    t = dot(lines[...], w[...]).astype(BF16)
    acc_t[...] = project(picked_value(t, pick_o), w, KV)
    pick_rows(t, pick_t, text)


def attend_kernel(
    flags,
    x,
    g,
    f,
    p,
    text,
    pick_o,
    pick_t,
    lines,
    wo,
    wt,
    acc_x,
    acc_g,
    acc_f,
    acc_p,
    acc_t,
    q_gain,
    k_gain,
    bias,
    att,
    dq,
    near_t,
    even_t,
    odd_t,
    kraw,
    keys,
):
    n = 4 * ROWS
    mine = acc_x[...] + project(x, wt, KVQ)
    d_att = (acc_g[...] + project(g, wt, LAST)).astype(BF16)
    behind = acc_f[...] + project(f, wt, KV)
    beside = acc_p[...] + project(p, wt, KV, part_order(flags))
    words = acc_t[...] + project(text, wt, KV)
    t = dot(lines[...], wt[...]).astype(BF16)
    more = project(picked_value(t, pick_o), wo, KV) + project(picked_value(t, pick_t), wt, KV)
    kraw[...] = mine[:, :W]
    low = 0
    for values in (mine, beside[:ROWS], behind, beside[ROWS:], words, more):
        high = low + values.shape[0]
        for h in range(NH):
            kn = norm_rows(values[:, head(h)], k_gain[:, head(h)])
            keys[low:high, head(h)] = kn.astype(BF16)
        keys[low:high, W:] = values[:, W : 2 * W].astype(BF16)
        low = high
    even = flags[0].astype(F32)
    odd = 1.0 - even
    for h in range(NH):
        q = mine[:, val(NH + h)]
        qh = norm_rows(q, q_gain[:, head(h)]).astype(BF16)
        dh = d_att[:, head(h)]
        kh = keys[:, head(h)]
        vh = keys[:, val(h)]
        s = dot(qh, kh, NT) * SCALE + bias[...]
        e = jnp.exp(s - jnp.max(s, axis=-1, keepdims=True))
        p_h = e * (1.0 / jnp.sum(e, axis=-1, keepdims=True))
        pb = p_h.astype(BF16)
        att[:, head(h)] = dot(pb, vh).astype(BF16)
        dp = dot(dh, vh, NT)
        ds = (p_h * (dp - jnp.sum(p_h * dp, axis=-1, keepdims=True))).astype(BF16)
        d_q = dot(ds, kh) * SCALE
        dq[:, head(h)] = norm_pull(q, q_gain[:, head(h)], d_q).astype(BF16)
        kt = dot(ds[:, :n], qh, TN) * SCALE
        vt = dot(pb[:, :n], dh, TN)
        for lanes, term in ((head(h), kt), (val(h), vt)):
            near_t[:, lanes] = term[: 2 * ROWS].astype(BF16)
            even_t[:, lanes] = (term[2 * ROWS :] * even).astype(BF16)
            odd_t[:, lanes] = (term[2 * ROWS :] * odd).astype(BF16)


def out_kernel(att, wo, wt, pick_o, pick_t, out):
    for j in range(4):
        rows = slice(j * PART, (j + 1) * PART)
        o = dot(att[...], wo[rows, LAST], NT).astype(BF16)
        t = dot(att[...], wt[rows, LAST], NT).astype(BF16)
        out[j] = (dot(o, pick_o[...], NT) + dot(t, pick_t[...], NT)).astype(BF16)


def term_kernel(flags, near_t, got_even, got_odd, own, to_mate, to_next):
    total = near_t[...].astype(F32) + got_even[...].astype(F32) + got_odd[...].astype(F32)
    own[...] = total[:ROWS]
    mate = flags[1].astype(F32)
    to_mate[...] = (total[ROWS:] * mate).astype(BF16)
    to_next[...] = (total[ROWS:] * (1.0 - mate)).astype(BF16)


def grad_kernel(own, in_a, in_b, kraw, k_gain, dq, wo, wt, pick_o, pick_t, out):
    total = own[...] + in_a[...].astype(F32) + in_b[...].astype(F32)
    parts = [
        norm_pull(kraw[:, head(h)], k_gain[:, head(h)], total[:, head(h)]).astype(BF16)
        for h in range(NH)
    ]
    d = jnp.concatenate(parts + [total[:, W:].astype(BF16), dq[...]], axis=1)
    for j in range(4):
        rows = slice(j * PART, (j + 1) * PART)
        o = dot(d, wo[rows, KVQ], NT).astype(BF16)
        t = dot(d, wt[rows, KVQ], NT).astype(BF16)
        out[j] = (dot(o, pick_o[...], NT) + dot(t, pick_t[...], NT)).astype(BF16)


def head_total(parts):
    return f32_sum(*[parts[n] for n in range(4)]).astype(BF16)


def f32_sum(*terms):
    total = terms[0].astype(F32)
    for term in terms[1:]:
        total = total + term.astype(F32)
    return total


def head_shift(value, by):
    return lax.ppermute(value, "heads", [(i, (i + by) % 4) for i in range(4)])


def per_device(
    x_tiles, x_text, w_query, w_key, w_value, w_output, q_gain, k_gain, text_mask, windows, grad_out
):
    place = lax.axis_index("seq")
    me = lax.axis_index("heads")
    core, x, col = place & 1, place >> 5, place & 31
    window = lax.dynamic_slice(windows, (place, jnp.int32(0)), (1, 2))
    use_even = (window[0, 0] == x) == ((x & 1) == 0)
    use_core = (window[0, 1] == col) == (core == 0)
    q_gain = q_gain[None, :]
    k_gain = k_gain[None, :]
    blocks = [(me - by) & 3 for by in range(4)]
    flags = jnp.stack([use_even.astype(jnp.int32), use_core.astype(jnp.int32)] + blocks)

    at = jnp.arange(PART, dtype=jnp.int32)
    inner = at % BLOCK
    feature = lax.broadcasted_iota(jnp.int32, (W, PART), 0)

    def pick(which):
        natural = ((inner // 12 * 4 + at // BLOCK) * 2 + which) * 12 + inner % 12
        hit = (feature == natural[None, :]) & (inner < 48)[None, :]
        return hit.astype(BF16)

    pick_o, pick_t = pick(core), pick(1 - core)
    t = jnp.arange(HALF_TEXT, dtype=jnp.int32)
    line = t // 8 * BLOCK + 48 + t % 8
    lines = (line[:, None] == jnp.arange(16 * BLOCK, dtype=jnp.int32)[None, :]).astype(BF16)
    t = jnp.arange(TEXT, dtype=jnp.int32)
    token = place_of(t // 32 % 4, t // 2 % 4, t // 8 % 4, (t // 128) ^ core) * 2 + t % 2
    valid = jnp.sum(jnp.where(t[:, None] == token[None, :], text_mask[:, None], 0), axis=0)
    bias = jnp.concatenate(
        [jnp.zeros((4 * ROWS,), F32), jnp.where(valid == 1, 0.0, -1e30).astype(F32)]
    )[None, :]

    quarter = lax.dynamic_slice(x_tiles, (jnp.int32(0), me * W), (ROWS, W))
    mine = jnp.concatenate([w_key, w_value, w_query, w_output], axis=1)
    four = over_zh(jnp.concatenate([mine, x_text], axis=0))
    behind = jnp.where(use_even, row_even(x_tiles), row_odd(x_tiles))
    side = jnp.where(use_core, core_mate(quarter), next_chip(quarter))
    side, behind, pick_o, pick_t, flags = lax.optimization_barrier(
        (side, behind, pick_o, pick_t, flags)
    )
    c_even, c_odd = row_even(side), row_odd(side)
    four, c_even, c_odd = lax.optimization_barrier((four, c_even, c_odd))
    corner = jnp.where(use_even, c_even, c_odd)
    beside = jnp.concatenate([side, corner])
    block = jnp.concatenate([four[:, :12].reshape(48, 1536), four[:, 12:].reshape(8, 1536)], axis=0)
    block, beside, lines, bias = lax.optimization_barrier((block, beside, lines, bias))
    parts = [beside] + [head_shift(beside, by) for by in (1, 2, 3)]
    wo = over_xy(block).reshape(16 * BLOCK, 1536)
    picked = shape((4, ROWS, PART), BF16)
    x_o, x_t, g_o, g_t, f_o, f_t = call(pick_kernel, (picked,) * 6, "v" * 5)(
        x_tiles, grad_out, behind, pick_o, pick_t
    )
    p_o, p_t = call(pick_parts_kernel, (shape((4, 2 * ROWS, PART), BF16),) * 2, "v" * 6)(
        *parts, pick_o, pick_t
    )
    wo, x_o, x_t, g_o, g_t, f_o, f_t, p_o, p_t = lax.optimization_barrier(
        (wo, x_o, x_t, g_o, g_t, f_o, f_t, p_o, p_t)
    )
    wt = core_mate(wo)

    *accs, text = call(
        first_kernel,
        (
            shape((ROWS, 3 * W), F32),
            shape((ROWS, W), F32),
            shape((ROWS, 2 * W), F32),
            shape((2 * ROWS, 2 * W), F32),
            shape((HALF_TEXT, 2 * W), F32),
            shape((4, HALF_TEXT, PART), BF16),
        ),
        "s" + "v" * 8,
    )(flags, x_o, g_o, f_o, p_o, pick_o, pick_t, lines, wo)
    att, dq, near_t, even_t, odd_t, kraw = call(
        attend_kernel,
        (
            shape((ROWS, W), BF16),
            shape((ROWS, W), BF16),
            shape((2 * ROWS, 768), BF16),
            shape((2 * ROWS, 768), BF16),
            shape((2 * ROWS, 768), BF16),
            shape((ROWS, W), F32),
        ),
        "s" + "v" * 18,
        scratch=[pltpu.VMEM((1024, 768), BF16)],
        mib=28,
    )(flags, x_t, g_t, f_t, p_t, text, pick_o, pick_t, lines, wo, wt, *accs, q_gain, k_gain, bias)

    got_even, got_odd = row_even(even_t), row_odd(odd_t)
    out = call(out_kernel, shape((4, ROWS, W), BF16), "v" * 5, flops=OUT_COST)(
        att, wo, wt, pick_o, pick_t
    )
    outs = lax.all_to_all(out, "heads", 0, 0)
    own_t, to_mate, to_next = call(
        term_kernel,
        (shape((ROWS, 768), F32), shape((ROWS, 768), BF16), shape((ROWS, 768), BF16)),
        "svvv",
        mib=8,
        flops=TERM_COST,
    )(flags, near_t, got_even, got_odd)
    mate_t, next_t = core_mate(to_mate), next_chip(to_next)
    grad = call(grad_kernel, shape((4, ROWS, W), BF16), "v" * 10, flops=GRAD_COST)(
        own_t, mate_t, next_t, kraw, k_gain, dq, wo, wt, pick_o, pick_t
    )
    grads = lax.all_to_all(grad, "heads", 0, 0)
    return (head_total(outs), head_total(grads))


def solution(mesh):
    in_specs = (
        P("seq", None),
        P("seq", None),
        P("seq", "heads"),
        P("seq", "heads"),
        P("seq", "heads"),
        P("seq", "heads"),
        P("heads"),
        P("heads"),
        P(),
        P(),
        P("seq", None),
    )
    out_specs = (P("seq", "heads"), P("seq", "heads"))
    return jax.shard_map(
        per_device, mesh=mesh, in_specs=in_specs, out_specs=out_specs, check_vma=False
    )
```

```python
import functools

import jax
import jax.numpy as jnp
from jax import lax
from jax.experimental import pallas as pl
from jax.experimental.pallas import tpu as pltpu
from jax.sharding import PartitionSpec as P

HD = 128
NH = 3
W = NH * HD
ROWS = 192
TEXT = 256
EPS = 1e-6
SCALE = HD**-0.5
OUT_COST = 10**9
TURN_COST = 10**11
GRAD_COST = 10**9
BLOCK = 56
PART = 4 * BLOCK
F32 = jnp.float32
BF16 = jnp.bfloat16
NT = (((1,), (1,)), ((), ()))
TN = (((0,), (0,)), ((), ()))


def place_of(x, zh, y, core):
    return ((x * 4 + zh) * 4 + y) * 2 + core


def all_places():
    return [(x, z, y, c) for x in range(4) for z in range(4) for y in range(4) for c in range(2)]


def seq_move(value, target):
    pairs = []
    for at in all_places():
        to = target(*at)
        if to is not None:
            pairs.append((place_of(*at), place_of(*to)))
    return lax.ppermute(value, "seq", pairs)


def core_mate(value):
    return seq_move(value, lambda x, z, y, c: (x, z, y, 1 - c))


def next_chip(value):
    def target(x, z, y, c):
        col = (z * 4 + y) * 2 + c
        col = col + 1 if c == 1 else col - 1
        if not 0 <= col < 32:
            return None
        return (x, col // 8, col // 2 % 4, col % 2)

    return seq_move(value, target)


def row_even(value):
    return seq_move(value, lambda x, z, y, c: (x ^ 1, z, y, c))


def row_odd(value):
    return seq_move(value, lambda x, z, y, c: (3 - x, z, y, c) if x in (1, 2) else None)


def give_all(value, groups):
    copies = jnp.broadcast_to(value[None], (len(groups[0]),) + value.shape)
    return lax.all_to_all(copies, "seq", 0, 0, axis_index_groups=groups)


def over_zh(value):
    four = range(4)
    return give_all(
        value,
        [[place_of(x, z, y, c) for z in four] for x in four for y in four for c in range(2)],
    )


def over_xy(value):
    four = range(4)
    return give_all(
        value,
        [[place_of(x, z, y, c) for x in four for y in four] for z in four for c in range(2)],
    )


def dot(a, b, dims=(((1,), (0,)), ((), ()))):
    return lax.dot_general(a, b, dims, preferred_element_type=F32)


def norm_rows(a, gain):
    r = lax.rsqrt(jnp.mean(a * a, axis=-1, keepdims=True) + EPS)
    return a * r * gain


def norm_pull(a, gain, dy):
    r = lax.rsqrt(jnp.mean(a * a, axis=-1, keepdims=True) + EPS)
    t = dy * gain
    return r * t - a * (r * r * r * jnp.mean(t * a, axis=-1, keepdims=True))


def head(h):
    return slice(h * HD, (h + 1) * HD)


def val(h):
    return slice(W + h * HD, W + (h + 1) * HD)


def call(kernel, outs, spaces, scratch=(), mib=16, flops=10**9):
    place = {"s": pltpu.SMEM, "h": pltpu.HBM, "v": pltpu.VMEM}
    return pl.pallas_call(
        kernel,
        out_shape=outs,
        in_specs=[pl.BlockSpec(memory_space=place[space]) for space in spaces],
        scratch_shapes=scratch,
        compiler_params=pltpu.CompilerParams(vmem_limit_bytes=mib * 2**20),
        cost_estimate=pl.CostEstimate(flops=flops, bytes_accessed=8 * 10**6, transcendentals=0),
    )


def shape(dims, dtype):
    return jax.ShapeDtypeStruct(dims, dtype)


KVQ = slice(0, 3 * W)
KV = slice(0, 2 * W)
LAST = slice(3 * W, 4 * W)
HALF_TEXT = TEXT // 2
OWN = slice(0, ROWS)
GIVEN = slice(ROWS, 2 * ROWS)
KRAW = slice(2 * ROWS, 3 * ROWS)
D_Q = slice(3 * ROWS, 4 * ROWS)
BEHIND = slice(2 * ROWS, 3 * ROWS)


def pick_kernel(x, g, f, pick_o, pick_t, out_o, out_t):
    for n, rows in enumerate((x, g, f)):
        at = slice(n * ROWS, (n + 1) * ROWS)
        for j in range(4):
            out_o[j, at] = dot(rows[:, j * W : (j + 1) * W], pick_o[...]).astype(BF16)
            out_t[j, at] = dot(rows[:, j * W : (j + 1) * W], pick_t[...]).astype(BF16)


def pick_parts_kernel(p0, p1, p2, p3, pick_o, pick_t, out_o, out_t):
    for n, part in enumerate((p0, p1, p2, p3)):
        out_o[n] = dot(part[...], pick_o[...]).astype(BF16)
        out_t[n] = dot(part[...], pick_t[...]).astype(BF16)


def project(picked, w, cols, order=(0, 1, 2, 3), at=slice(None)):
    acc = None
    for n, j in enumerate(order):
        if isinstance(j, int):
            rows = w[j * PART : (j + 1) * PART, cols]
        else:
            rows = w[pl.ds(pl.multiple_of(j * PART, PART), PART), cols]
        term = dot(picked[n][at] if isinstance(picked, list) else picked[n, at], rows)
        acc = term if acc is None else acc + term
    return acc


def picked_value(rows, pick):
    return [dot(rows[:, j * W : (j + 1) * W], pick[...]).astype(BF16) for j in range(4)]


def part_order(flags):
    return [flags[2 + n] for n in range(4)]


def first_kernel(
    flags, r, p, pick_o, pick_t, lines, w, acc_x, acc_g, acc_f, acc_p, acc_t, text
):
    acc_x[...] = project(r, w, KVQ, at=OWN)
    acc_g[...] = project(r, w, LAST, at=GIVEN)
    acc_f[...] = project(r, w, KV, at=BEHIND)
    acc_p[...] = project(p, w, KV, part_order(flags))
    t = dot(lines[...], w[...]).astype(BF16)
    acc_t[...] = project(picked_value(t, pick_o), w, KV)
    for j, rows in enumerate(picked_value(t, pick_t)):
        text[j] = rows


def attend_kernel(
    flags,
    r,
    p,
    text,
    pick_o,
    pick_t,
    lines,
    wo,
    wt,
    acc_x,
    acc_g,
    acc_f,
    acc_p,
    acc_t,
    q_gain,
    k_gain,
    bias,
    att,
    keep,
    even_t,
    odd_t,
    keys,
):
    n = 4 * ROWS
    mine = acc_x[...] + project(r, wt, KVQ, at=OWN)
    d_att = (acc_g[...] + project(r, wt, LAST, at=GIVEN)).astype(BF16)
    behind = acc_f[...] + project(r, wt, KV, at=BEHIND)
    beside = acc_p[...] + project(p, wt, KV, part_order(flags))
    words = acc_t[...] + project(text, wt, KV)
    t = dot(lines[...], wt[...]).astype(BF16)
    more = project(picked_value(t, pick_o), wo, KV) + project(picked_value(t, pick_t), wt, KV)
    high = mine[:, :W].astype(BF16)
    keep[KRAW, :W] = high
    keep[KRAW, W:] = (mine[:, :W] - high.astype(F32)).astype(BF16)
    keep[D_Q, W:] = jnp.zeros((ROWS, W), BF16)
    low = 0
    for values in (mine, beside[:ROWS], behind, beside[ROWS:], words, more):
        high = low + values.shape[0]
        for h in range(NH):
            kn = norm_rows(values[:, head(h)], k_gain[:, head(h)])
            keys[low:high, head(h)] = kn.astype(BF16)
        keys[low:high, W:] = values[:, W : 2 * W].astype(BF16)
        low = high
    even = flags[0].astype(F32)
    odd = 1.0 - even
    for h in range(NH):
        q = mine[:, val(NH + h)]
        qh = norm_rows(q, q_gain[:, head(h)]).astype(BF16)
        dh = d_att[:, head(h)]
        kh = keys[:, head(h)]
        vh = keys[:, val(h)]
        s = dot(qh, kh, NT) * SCALE + bias[...]
        e = jnp.exp(s - jnp.max(s, axis=-1, keepdims=True))
        p_h = e * (1.0 / jnp.sum(e, axis=-1, keepdims=True))
        pb = p_h.astype(BF16)
        att[:, head(h)] = dot(pb, vh).astype(BF16)
        dp = dot(dh, vh, NT)
        ds = (p_h * (dp - jnp.sum(p_h * dp, axis=-1, keepdims=True))).astype(BF16)
        d_q = dot(ds, kh) * SCALE
        keep[D_Q, head(h)] = norm_pull(q, q_gain[:, head(h)], d_q).astype(BF16)
        kt = dot(ds[:, :n], qh, TN) * SCALE
        vt = dot(pb[:, :n], dh, TN)
        for lanes, term in ((head(h), kt), (val(h), vt)):
            keep[: 2 * ROWS, lanes] = term[: 2 * ROWS].astype(BF16)
            even_t[:, lanes] = (term[2 * ROWS :] * even).astype(BF16)
            odd_t[:, lanes] = (term[2 * ROWS :] * odd).astype(BF16)


def out_kernel(att, wo, wt, pick_o, pick_t, out):
    for j in range(4):
        rows = slice(j * PART, (j + 1) * PART)
        o = dot(att[...], wo[rows, LAST], NT).astype(BF16)
        t = dot(att[...], wt[rows, LAST], NT).astype(BF16)
        out[j] = (dot(o, pick_o[...], NT) + dot(t, pick_t[...], NT)).astype(BF16)


def turn_kernel(flags, keep, got_even, got_odd, own, to_next, to_mate):
    total = keep[: 2 * ROWS, :].astype(F32) + got_even[...].astype(F32) + got_odd[...].astype(F32)
    own[...] = total[:ROWS]
    mate = flags[1].astype(F32)
    to_next[...] = (total[ROWS:] * (1.0 - mate)).astype(BF16)
    to_mate[...] = (total[ROWS:] * mate).astype(BF16)


def grad_kernel(own, from_next, from_mate, keep, k_gain, wo, wt, pick_o, pick_t, out):
    total = own[...] + from_next[...].astype(F32) + from_mate[...].astype(F32)
    kraw = keep[KRAW, :W].astype(F32) + keep[KRAW, W:].astype(F32)
    parts = [
        norm_pull(kraw[:, head(h)], k_gain[:, head(h)], total[:, head(h)]).astype(BF16)
        for h in range(NH)
    ]
    d = jnp.concatenate(parts + [total[:, W:].astype(BF16), keep[D_Q, :W]], axis=1)
    for j in range(4):
        rows = slice(j * PART, (j + 1) * PART)
        o = dot(d, wo[rows, KVQ], NT).astype(BF16)
        t = dot(d, wt[rows, KVQ], NT).astype(BF16)
        out[j] = (dot(o, pick_o[...], NT) + dot(t, pick_t[...], NT)).astype(BF16)


def head_total(parts):
    return f32_sum(*[parts[n] for n in range(4)]).astype(BF16)


def f32_sum(*terms):
    total = terms[0].astype(F32)
    for term in terms[1:]:
        total = total + term.astype(F32)
    return total


def head_shift(value, by):
    return lax.ppermute(value, "heads", [(i, (i + by) % 4) for i in range(4)])


def per_device(
    x_tiles, x_text, w_query, w_key, w_value, w_output, q_gain, k_gain, text_mask, windows, grad_out
):
    place = lax.axis_index("seq")
    me = lax.axis_index("heads")
    core, x, col = place & 1, place >> 5, place & 31
    window = lax.dynamic_slice(windows, (place, jnp.int32(0)), (1, 2))
    use_even = (window[0, 0] == x) == ((x & 1) == 0)
    use_core = (window[0, 1] == col) == (core == 0)
    q_gain = q_gain[None, :]
    k_gain = k_gain[None, :]
    blocks = [(me - by) & 3 for by in range(4)]
    flags = jnp.stack([use_even.astype(jnp.int32), use_core.astype(jnp.int32)] + blocks)

    at = jnp.arange(PART, dtype=jnp.int32)
    inner = at % BLOCK
    feature = lax.broadcasted_iota(jnp.int32, (W, PART), 0)

    def pick(which):
        natural = ((inner // 12 * 4 + at // BLOCK) * 2 + which) * 12 + inner % 12
        hit = (feature == natural[None, :]) & (inner < 48)[None, :]
        return hit.astype(BF16)

    pick_o, pick_t = pick(core), pick(1 - core)
    t = jnp.arange(HALF_TEXT, dtype=jnp.int32)
    line = t // 8 * BLOCK + 48 + t % 8
    lines = (line[:, None] == jnp.arange(16 * BLOCK, dtype=jnp.int32)[None, :]).astype(BF16)
    t = jnp.arange(TEXT, dtype=jnp.int32)
    token = place_of(t // 32 % 4, t // 2 % 4, t // 8 % 4, (t // 128) ^ core) * 2 + t % 2
    valid = jnp.sum(jnp.where(t[:, None] == token[None, :], text_mask[:, None], 0), axis=0)
    bias = jnp.concatenate(
        [jnp.zeros((4 * ROWS,), F32), jnp.where(valid == 1, 0.0, -1e30).astype(F32)]
    )[None, :]

    quarter = lax.dynamic_slice(x_tiles, (jnp.int32(0), me * W), (ROWS, W))
    mine = jnp.concatenate([w_key, w_value, w_query, w_output], axis=1)
    four = over_zh(jnp.concatenate([mine, x_text], axis=0))
    behind = jnp.where(use_even, row_even(x_tiles), row_odd(x_tiles))
    side = jnp.where(use_core, core_mate(quarter), next_chip(quarter))
    side, behind = lax.optimization_barrier((side, behind))
    c_even, c_odd = row_even(side), row_odd(side)
    four, c_even, c_odd = lax.optimization_barrier((four, c_even, c_odd))
    corner = jnp.where(use_even, c_even, c_odd)
    beside = jnp.concatenate([side, corner])
    block = jnp.concatenate([four[:, :12].reshape(48, 1536), four[:, 12:].reshape(8, 1536)], axis=0)
    block, beside = lax.optimization_barrier((block, beside))
    parts = [beside] + [head_shift(beside, by) for by in (1, 2, 3)]
    wo = over_xy(block).reshape(16 * BLOCK, 1536)
    r_o, r_t = call(pick_kernel, (shape((4, 3 * ROWS, PART), BF16),) * 2, "v" * 5)(
        x_tiles, grad_out, behind, pick_o, pick_t
    )
    p_o, p_t = call(pick_parts_kernel, (shape((4, 2 * ROWS, PART), BF16),) * 2, "v" * 6)(
        *parts, pick_o, pick_t
    )
    wo, r_o, r_t, p_o, p_t, lines, bias, flags = lax.optimization_barrier(
        (wo, r_o, r_t, p_o, p_t, lines, bias, flags)
    )
    wt = core_mate(wo)

    *accs, text = call(
        first_kernel,
        (
            shape((ROWS, 3 * W), F32),
            shape((ROWS, W), F32),
            shape((ROWS, 2 * W), F32),
            shape((2 * ROWS, 2 * W), F32),
            shape((HALF_TEXT, 2 * W), F32),
            shape((4, HALF_TEXT, PART), BF16),
        ),
        "s" + "v" * 6,
    )(flags, r_o, p_o, pick_o, pick_t, lines, wo)
    att, keep, *terms = call(
        attend_kernel,
        (
            shape((ROWS, W), BF16),
            shape((4 * ROWS, 2 * W), BF16),
            *[shape((2 * ROWS, 2 * W), BF16)] * 2,
        ),
        "s" + "v" * 16,
        scratch=[pltpu.VMEM((1024, 768), BF16)],
        mib=28,
    )(flags, r_t, p_t, text, pick_o, pick_t, lines, wo, wt, *accs, q_gain, k_gain, bias)

    out = call(out_kernel, shape((4, ROWS, W), BF16), "v" * 5, flops=OUT_COST)(
        att, wo, wt, pick_o, pick_t
    )
    outs = lax.all_to_all(out, "heads", 0, 0)

    even_t, odd_t = terms
    own, to_next, to_mate = call(
        turn_kernel,
        (shape((ROWS, 2 * W), F32), *[shape((ROWS, 2 * W), BF16)] * 2),
        "svvv",
        mib=8,
        flops=TURN_COST,
    )(flags, keep, row_even(even_t), row_odd(odd_t))
    grad = call(grad_kernel, shape((4, ROWS, W), BF16), "v" * 9, flops=GRAD_COST)(
        own, next_chip(to_next), core_mate(to_mate), keep, k_gain, wo, wt, pick_o, pick_t
    )
    grads = lax.all_to_all(grad, "heads", 0, 0)
    return (head_total(outs), head_total(grads))


def solution(mesh):
    in_specs = (
        P("seq", None),
        P("seq", None),
        P("seq", "heads"),
        P("seq", "heads"),
        P("seq", "heads"),
        P("seq", "heads"),
        P("heads"),
        P("heads"),
        P(),
        P(),
        P("seq", None),
    )
    out_specs = (P("seq", "heads"), P("seq", "heads"))
    return jax.shard_map(
        per_device, mesh=mesh, in_specs=in_specs, out_specs=out_specs, check_vma=False
    )
```

```python
import functools

import jax
import jax.numpy as jnp
from jax import lax
from jax.experimental import pallas as pl
from jax.experimental.pallas import tpu as pltpu
from jax.sharding import PartitionSpec as P

HD = 128
NH = 3
W = NH * HD
ROWS = 192
TEXT = 256
EPS = 1e-6
SCALE = HD**-0.5
OUT_COST = 10**9
TURN_COST = 10**11
GRAD_COST = 10**9
BLOCK = 56
PART = 4 * BLOCK
F32 = jnp.float32
BF16 = jnp.bfloat16
NT = (((1,), (1,)), ((), ()))
TN = (((0,), (0,)), ((), ()))


def place_of(x, zh, y, core):
    return ((x * 4 + zh) * 4 + y) * 2 + core


def all_places():
    return [(x, z, y, c) for x in range(4) for z in range(4) for y in range(4) for c in range(2)]


def seq_move(value, target):
    pairs = []
    for at in all_places():
        to = target(*at)
        if to is not None:
            pairs.append((place_of(*at), place_of(*to)))
    return lax.ppermute(value, "seq", pairs)


def core_mate(value):
    return seq_move(value, lambda x, z, y, c: (x, z, y, 1 - c))


def next_chip(value):
    def target(x, z, y, c):
        col = (z * 4 + y) * 2 + c
        col = col + 1 if c == 1 else col - 1
        if not 0 <= col < 32:
            return None
        return (x, col // 8, col // 2 % 4, col % 2)

    return seq_move(value, target)


def row_even(value):
    return seq_move(value, lambda x, z, y, c: (x ^ 1, z, y, c))


def row_odd(value):
    return seq_move(value, lambda x, z, y, c: (3 - x, z, y, c) if x in (1, 2) else None)


def give_all(value, groups):
    copies = jnp.broadcast_to(value[None], (len(groups[0]),) + value.shape)
    return lax.all_to_all(copies, "seq", 0, 0, axis_index_groups=groups)


def over_zh(value):
    four = range(4)
    return give_all(
        value,
        [[place_of(x, z, y, c) for z in four] for x in four for y in four for c in range(2)],
    )


def over_xy(value):
    four = range(4)
    return give_all(
        value,
        [[place_of(x, z, y, c) for x in four for y in four] for z in four for c in range(2)],
    )


def dot(a, b, dims=(((1,), (0,)), ((), ()))):
    return lax.dot_general(a, b, dims, preferred_element_type=F32)


def norm_rows(a, gain):
    r = lax.rsqrt(jnp.mean(a * a, axis=-1, keepdims=True) + EPS)
    return a * r * gain


def norm_pull(a, gain, dy):
    r = lax.rsqrt(jnp.mean(a * a, axis=-1, keepdims=True) + EPS)
    t = dy * gain
    return r * t - a * (r * r * r * jnp.mean(t * a, axis=-1, keepdims=True))


def head(h):
    return slice(h * HD, (h + 1) * HD)


def val(h):
    return slice(W + h * HD, W + (h + 1) * HD)


def call(kernel, outs, spaces, scratch=(), mib=16, flops=10**9):
    place = {"s": pltpu.SMEM, "h": pltpu.HBM, "v": pltpu.VMEM}
    return pl.pallas_call(
        kernel,
        out_shape=outs,
        in_specs=[pl.BlockSpec(memory_space=place[space]) for space in spaces],
        scratch_shapes=scratch,
        compiler_params=pltpu.CompilerParams(vmem_limit_bytes=mib * 2**20),
        cost_estimate=pl.CostEstimate(flops=flops, bytes_accessed=8 * 10**6, transcendentals=0),
    )


def shape(dims, dtype):
    return jax.ShapeDtypeStruct(dims, dtype)


KVQ = slice(0, 3 * W)
KV = slice(0, 2 * W)
LAST = slice(3 * W, 4 * W)
HALF_TEXT = TEXT // 2
OWN = slice(0, ROWS)
GIVEN = slice(ROWS, 2 * ROWS)
KRAW = slice(2 * ROWS, 3 * ROWS)
D_Q = slice(3 * ROWS, 4 * ROWS)
BEHIND = slice(2 * ROWS, 3 * ROWS)


def pick_kernel(x, g, f, pick_o, pick_t, out_o, out_t):
    for n, rows in enumerate((x, g, f)):
        at = slice(n * ROWS, (n + 1) * ROWS)
        for j in range(4):
            out_o[j, at] = dot(rows[:, j * W : (j + 1) * W], pick_o[...]).astype(BF16)
            out_t[j, at] = dot(rows[:, j * W : (j + 1) * W], pick_t[...]).astype(BF16)


def pick_parts_kernel(p0, p1, p2, p3, pick_o, pick_t, out_o, out_t):
    for n, part in enumerate((p0, p1, p2, p3)):
        out_o[n] = dot(part[...], pick_o[...]).astype(BF16)
        out_t[n] = dot(part[...], pick_t[...]).astype(BF16)


def project(picked, w, cols, order=(0, 1, 2, 3), at=slice(None)):
    acc = None
    for n, j in enumerate(order):
        if isinstance(j, int):
            rows = w[j * PART : (j + 1) * PART, cols]
        else:
            rows = w[pl.ds(pl.multiple_of(j * PART, PART), PART), cols]
        term = dot(picked[n][at] if isinstance(picked, list) else picked[n, at], rows)
        acc = term if acc is None else acc + term
    return acc


def picked_value(rows, pick):
    return [dot(rows[:, j * W : (j + 1) * W], pick[...]).astype(BF16) for j in range(4)]


def part_order(flags):
    return [flags[2 + n] for n in range(4)]


def first_kernel(
    flags, r, p, pick_o, pick_t, lines, w, acc_x, acc_g, acc_f, acc_p, acc_t, text
):
    acc_x[...] = project(r, w, KVQ, at=OWN)
    acc_g[...] = project(r, w, LAST, at=GIVEN)
    acc_f[...] = project(r, w, KV, at=BEHIND)
    acc_p[...] = project(p, w, KV, part_order(flags))
    t = dot(lines[...], w[...]).astype(BF16)
    acc_t[...] = project(picked_value(t, pick_o), w, KV)
    for j, rows in enumerate(picked_value(t, pick_t)):
        text[j] = rows


def attend_kernel(
    flags,
    r,
    p,
    text,
    pick_o,
    pick_t,
    lines,
    wo,
    wt,
    acc_x,
    acc_g,
    acc_f,
    acc_p,
    acc_t,
    q_gain,
    k_gain,
    bias,
    att,
    keep,
    even_t,
    odd_t,
    keys,
):
    n = 4 * ROWS
    mine = acc_x[...] + project(r, wt, KVQ, at=OWN)
    d_att = (acc_g[...] + project(r, wt, LAST, at=GIVEN)).astype(BF16)
    behind = acc_f[...] + project(r, wt, KV, at=BEHIND)
    beside = acc_p[...] + project(p, wt, KV, part_order(flags))
    words = acc_t[...] + project(text, wt, KV)
    t = dot(lines[...], wt[...]).astype(BF16)
    more = project(picked_value(t, pick_o), wo, KV) + project(picked_value(t, pick_t), wt, KV)
    high = mine[:, :W].astype(BF16)
    keep[KRAW, :W] = high
    keep[KRAW, W:] = (mine[:, :W] - high.astype(F32)).astype(BF16)
    keep[D_Q, W:] = jnp.zeros((ROWS, W), BF16)
    low = 0
    for values in (mine, beside[:ROWS], behind, beside[ROWS:], words, more):
        high = low + values.shape[0]
        for h in range(NH):
            kn = norm_rows(values[:, head(h)], k_gain[:, head(h)])
            keys[low:high, head(h)] = kn.astype(BF16)
        keys[low:high, W:] = values[:, W : 2 * W].astype(BF16)
        low = high
    even = flags[0].astype(F32)
    odd = 1.0 - even
    for h in range(NH):
        q = mine[:, val(NH + h)]
        qh = norm_rows(q, q_gain[:, head(h)]).astype(BF16)
        dh = d_att[:, head(h)]
        kh = keys[:, head(h)]
        vh = keys[:, val(h)]
        s = dot(qh, kh, NT) * SCALE + bias[...]
        e = jnp.exp(s - jnp.max(s, axis=-1, keepdims=True))
        p_h = e * (1.0 / jnp.sum(e, axis=-1, keepdims=True))
        pb = p_h.astype(BF16)
        att[:, head(h)] = dot(pb, vh).astype(BF16)
        dp = dot(dh, vh, NT)
        ds = (p_h * (dp - jnp.sum(p_h * dp, axis=-1, keepdims=True))).astype(BF16)
        d_q = dot(ds, kh) * SCALE
        keep[D_Q, head(h)] = norm_pull(q, q_gain[:, head(h)], d_q).astype(BF16)
        kt = dot(ds[:, :n], qh, TN) * SCALE
        vt = dot(pb[:, :n], dh, TN)
        for lanes, term in ((head(h), kt), (val(h), vt)):
            keep[: 2 * ROWS, lanes] = term[: 2 * ROWS].astype(BF16)
            even_t[:, lanes] = (term[2 * ROWS :] * even).astype(BF16)
            odd_t[:, lanes] = (term[2 * ROWS :] * odd).astype(BF16)


def out_kernel(att, wo, wt, pick_o, pick_t, out):
    for j in range(4):
        rows = slice(j * PART, (j + 1) * PART)
        o = dot(att[...], wo[rows, LAST], NT).astype(BF16)
        t = dot(att[...], wt[rows, LAST], NT).astype(BF16)
        out[j] = (dot(o, pick_o[...], NT) + dot(t, pick_t[...], NT)).astype(BF16)


def turn_kernel(flags, keep, got_even, got_odd, own, to_next, to_mate):
    total = keep[: 2 * ROWS, :].astype(F32) + got_even[...].astype(F32) + got_odd[...].astype(F32)
    own[...] = total[:ROWS]
    mate = flags[1].astype(F32)
    to_next[...] = (total[ROWS:] * (1.0 - mate)).astype(BF16)
    to_mate[...] = (total[ROWS:] * mate).astype(BF16)


def grad_kernel(own, from_next, from_mate, keep, k_gain, wo, wt, pick_o, pick_t, out):
    total = own[...] + from_next[...].astype(F32) + from_mate[...].astype(F32)
    kraw = keep[KRAW, :W].astype(F32) + keep[KRAW, W:].astype(F32)
    parts = [
        norm_pull(kraw[:, head(h)], k_gain[:, head(h)], total[:, head(h)]).astype(BF16)
        for h in range(NH)
    ]
    d = jnp.concatenate(parts + [total[:, W:].astype(BF16), keep[D_Q, :W]], axis=1)
    for j in range(4):
        rows = slice(j * PART, (j + 1) * PART)
        o = dot(d, wo[rows, KVQ], NT).astype(BF16)
        t = dot(d, wt[rows, KVQ], NT).astype(BF16)
        out[j] = (dot(o, pick_o[...], NT) + dot(t, pick_t[...], NT)).astype(BF16)


def head_total(parts):
    return f32_sum(*[parts[n] for n in range(4)]).astype(BF16)


def f32_sum(*terms):
    total = terms[0].astype(F32)
    for term in terms[1:]:
        total = total + term.astype(F32)
    return total


def head_shift(value, by):
    return lax.ppermute(value, "heads", [(i, (i + by) % 4) for i in range(4)])


def per_device(
    x_tiles, x_text, w_query, w_key, w_value, w_output, q_gain, k_gain, text_mask, windows, grad_out
):
    place = lax.axis_index("seq")
    me = lax.axis_index("heads")
    core, x, col = place & 1, place >> 5, place & 31
    window = lax.dynamic_slice(windows, (place, jnp.int32(0)), (1, 2))
    use_even = (window[:, :1] == x) == ((x & 1) == 0)
    use_core = (window[:, 1:] == col) == (core == 0)
    q_gain = q_gain[None, :]
    k_gain = k_gain[None, :]
    blocks = [(me - by) & 3 for by in range(4)]
    flags = jnp.stack([use_even[0, 0].astype(jnp.int32), use_core[0, 0].astype(jnp.int32)] + blocks)

    at = jnp.arange(PART, dtype=jnp.int32)
    inner = at % BLOCK
    feature = lax.broadcasted_iota(jnp.int32, (W, PART), 0)

    def pick(which):
        natural = ((inner // 12 * 4 + at // BLOCK) * 2 + which) * 12 + inner % 12
        hit = (feature == natural[None, :]) & (inner < 48)[None, :]
        return hit.astype(BF16)

    pick_o, pick_t = pick(core), pick(1 - core)
    t = jnp.arange(HALF_TEXT, dtype=jnp.int32)
    line = t // 8 * BLOCK + 48 + t % 8
    lines = (line[:, None] == jnp.arange(16 * BLOCK, dtype=jnp.int32)[None, :]).astype(BF16)
    t = jnp.arange(TEXT, dtype=jnp.int32)
    token = place_of(t // 32 % 4, t // 2 % 4, t // 8 % 4, (t // 128) ^ core) * 2 + t % 2
    valid = jnp.sum(jnp.where(t[:, None] == token[None, :], text_mask[:, None], 0), axis=0)
    bias = jnp.concatenate(
        [jnp.zeros((4 * ROWS,), F32), jnp.where(valid == 1, 0.0, -1e30).astype(F32)]
    )[None, :]

    quarter = lax.dynamic_slice(x_tiles, (jnp.int32(0), me * W), (ROWS, W))
    mine = jnp.concatenate([w_key, w_value, w_query, w_output], axis=1)
    four = over_zh(jnp.concatenate([mine, x_text], axis=0))
    behind = jnp.where(use_even, row_even(x_tiles), row_odd(x_tiles))
    side = jnp.where(use_core, core_mate(quarter), next_chip(quarter))
    side, behind = lax.optimization_barrier((side, behind))
    c_even, c_odd = row_even(side), row_odd(side)
    four, c_even, c_odd = lax.optimization_barrier((four, c_even, c_odd))
    corner = jnp.where(use_even, c_even, c_odd)
    beside = jnp.concatenate([side, corner])
    block = jnp.concatenate([four[:, :12].reshape(48, 1536), four[:, 12:].reshape(8, 1536)], axis=0)
    parts = [beside] + [head_shift(beside, by) for by in (1, 2, 3)]
    wo = over_xy(block).reshape(16 * BLOCK, 1536)
    r_o, r_t = call(pick_kernel, (shape((4, 3 * ROWS, PART), BF16),) * 2, "v" * 5)(
        x_tiles, grad_out, behind, pick_o, pick_t
    )
    p_o, p_t = call(pick_parts_kernel, (shape((4, 2 * ROWS, PART), BF16),) * 2, "v" * 6)(
        *parts, pick_o, pick_t
    )
    wo, r_o, r_t, p_o, p_t, lines, bias, flags = lax.optimization_barrier(
        (wo, r_o, r_t, p_o, p_t, lines, bias, flags)
    )
    wt = core_mate(wo)

    *accs, text = call(
        first_kernel,
        (
            shape((ROWS, 3 * W), F32),
            shape((ROWS, W), F32),
            shape((ROWS, 2 * W), F32),
            shape((2 * ROWS, 2 * W), F32),
            shape((HALF_TEXT, 2 * W), F32),
            shape((4, HALF_TEXT, PART), BF16),
        ),
        "s" + "v" * 6,
    )(flags, r_o, p_o, pick_o, pick_t, lines, wo)
    att, keep, *terms = call(
        attend_kernel,
        (
            shape((ROWS, W), BF16),
            shape((4 * ROWS, 2 * W), BF16),
            *[shape((2 * ROWS, 2 * W), BF16)] * 2,
        ),
        "s" + "v" * 16,
        scratch=[pltpu.VMEM((1024, 768), BF16)],
        mib=28,
    )(flags, r_t, p_t, text, pick_o, pick_t, lines, wo, wt, *accs, q_gain, k_gain, bias)

    out = call(out_kernel, shape((4, ROWS, W), BF16), "v" * 5, flops=OUT_COST)(
        att, wo, wt, pick_o, pick_t
    )
    outs = lax.all_to_all(out, "heads", 0, 0)

    even_t, odd_t = terms
    own, to_next, to_mate = call(
        turn_kernel,
        (shape((ROWS, 2 * W), F32), *[shape((ROWS, 2 * W), BF16)] * 2),
        "svvv",
        mib=8,
        flops=TURN_COST,
    )(flags, keep, row_even(even_t), row_odd(odd_t))
    grad = call(grad_kernel, shape((4, ROWS, W), BF16), "v" * 9, flops=GRAD_COST)(
        own, next_chip(to_next), core_mate(to_mate), keep, k_gain, wo, wt, pick_o, pick_t
    )
    grads = lax.all_to_all(grad, "heads", 0, 0)
    return (head_total(outs), head_total(grads))


def solution(mesh):
    in_specs = (
        P("seq", None),
        P("seq", None),
        P("seq", "heads"),
        P("seq", "heads"),
        P("seq", "heads"),
        P("seq", "heads"),
        P("heads"),
        P("heads"),
        P(),
        P(),
        P("seq", None),
    )
    out_specs = (P("seq", "heads"), P("seq", "heads"))
    return jax.shard_map(
        per_device, mesh=mesh, in_specs=in_specs, out_specs=out_specs, check_vma=False
    )
```

```python
import functools

import jax
import jax.numpy as jnp
from jax import lax
from jax.experimental import pallas as pl
from jax.experimental.pallas import tpu as pltpu
from jax.sharding import PartitionSpec as P

HD = 128
NH = 3
W = NH * HD
ROWS = 192
TEXT = 256
EPS = 1e-6
SCALE = HD**-0.5
OUT_COST = 10**9
TURN_COST = 10**11
GRAD_COST = 10**9
BLOCK = 56
PART = 4 * BLOCK
F32 = jnp.float32
BF16 = jnp.bfloat16
NT = (((1,), (1,)), ((), ()))
TN = (((0,), (0,)), ((), ()))


def place_of(x, zh, y, core):
    return ((x * 4 + zh) * 4 + y) * 2 + core


def all_places():
    return [(x, z, y, c) for x in range(4) for z in range(4) for y in range(4) for c in range(2)]


def seq_move(value, target):
    pairs = []
    for at in all_places():
        to = target(*at)
        if to is not None:
            pairs.append((place_of(*at), place_of(*to)))
    return lax.ppermute(value, "seq", pairs)


def core_mate(value):
    return seq_move(value, lambda x, z, y, c: (x, z, y, 1 - c))


def next_chip(value):
    def target(x, z, y, c):
        col = (z * 4 + y) * 2 + c
        col = col + 1 if c == 1 else col - 1
        if not 0 <= col < 32:
            return None
        return (x, col // 8, col // 2 % 4, col % 2)

    return seq_move(value, target)


def row_even(value):
    return seq_move(value, lambda x, z, y, c: (x ^ 1, z, y, c))


def row_odd(value):
    return seq_move(value, lambda x, z, y, c: (3 - x, z, y, c) if x in (1, 2) else None)


def give_all(value, groups):
    copies = jnp.broadcast_to(value[None], (len(groups[0]),) + value.shape)
    return lax.all_to_all(copies, "seq", 0, 0, axis_index_groups=groups)


def over_zh(value):
    four = range(4)
    return give_all(
        value,
        [[place_of(x, z, y, c) for z in four] for x in four for y in four for c in range(2)],
    )


def over_xy(value):
    four = range(4)
    return give_all(
        value,
        [[place_of(x, z, y, c) for x in four for y in four] for z in four for c in range(2)],
    )


def dot(a, b, dims=(((1,), (0,)), ((), ()))):
    return lax.dot_general(a, b, dims, preferred_element_type=F32)


def norm_rows(a, gain):
    r = lax.rsqrt(jnp.mean(a * a, axis=-1, keepdims=True) + EPS)
    return a * r * gain


def norm_pull(a, gain, dy):
    r = lax.rsqrt(jnp.mean(a * a, axis=-1, keepdims=True) + EPS)
    t = dy * gain
    return r * t - a * (r * r * r * jnp.mean(t * a, axis=-1, keepdims=True))


def head(h):
    return slice(h * HD, (h + 1) * HD)


def val(h):
    return slice(W + h * HD, W + (h + 1) * HD)


def call(kernel, outs, spaces, scratch=(), mib=16, flops=10**9):
    place = {"s": pltpu.SMEM, "h": pltpu.HBM, "v": pltpu.VMEM}
    return pl.pallas_call(
        kernel,
        out_shape=outs,
        in_specs=[pl.BlockSpec(memory_space=place[space]) for space in spaces],
        scratch_shapes=scratch,
        compiler_params=pltpu.CompilerParams(vmem_limit_bytes=mib * 2**20),
        cost_estimate=pl.CostEstimate(flops=flops, bytes_accessed=8 * 10**6, transcendentals=0),
    )


def shape(dims, dtype):
    return jax.ShapeDtypeStruct(dims, dtype)


KVQ = slice(0, 3 * W)
KV = slice(0, 2 * W)
LAST = slice(3 * W, 4 * W)
HALF_TEXT = TEXT // 2
OWN = slice(0, ROWS)
GIVEN = slice(ROWS, 2 * ROWS)
KRAW = slice(2 * ROWS, 3 * ROWS)
D_Q = slice(3 * ROWS, 4 * ROWS)
BEHIND = slice(2 * ROWS, 3 * ROWS)


def pick_kernel(x, g, f, pick_o, pick_t, out_o, out_t):
    for n, rows in enumerate((x, g, f)):
        at = slice(n * ROWS, (n + 1) * ROWS)
        for j in range(4):
            out_o[j, at] = dot(rows[:, j * W : (j + 1) * W], pick_o[...]).astype(BF16)
            out_t[j, at] = dot(rows[:, j * W : (j + 1) * W], pick_t[...]).astype(BF16)


def pick_parts_kernel(p0, p1, p2, p3, pick_o, pick_t, out_o, out_t):
    for n, part in enumerate((p0, p1, p2, p3)):
        out_o[n] = dot(part[...], pick_o[...]).astype(BF16)
        out_t[n] = dot(part[...], pick_t[...]).astype(BF16)


def project(picked, w, cols, order=(0, 1, 2, 3), at=slice(None)):
    acc = None
    for n, j in enumerate(order):
        if isinstance(j, int):
            rows = w[j * PART : (j + 1) * PART, cols]
        else:
            rows = w[pl.ds(pl.multiple_of(j * PART, PART), PART), cols]
        term = dot(picked[n][at] if isinstance(picked, list) else picked[n, at], rows)
        acc = term if acc is None else acc + term
    return acc


def text_rows(lines, w):
    parts = [dot(lines[...], w[j * PART : (j + 1) * PART, :]) for j in range(4)]
    return jnp.concatenate(parts, axis=0).astype(BF16)


def picked_value(rows, pick):
    return [dot(rows[:, j * W : (j + 1) * W], pick[...]).astype(BF16) for j in range(4)]


def part_order(flags):
    return [flags[2 + n] for n in range(4)]


def first_kernel(
    flags, r, p, pick_o, pick_t, lines, w, acc_x, acc_g, acc_f, acc_p, acc_t, text
):
    acc_x[...] = project(r, w, KVQ, at=OWN)
    acc_g[...] = project(r, w, LAST, at=GIVEN)
    acc_f[...] = project(r, w, KV, at=BEHIND)
    acc_p[...] = project(p, w, KV, part_order(flags))
    t = text_rows(lines, w)
    acc_t[...] = project(picked_value(t, pick_o), w, KV)
    for j, rows in enumerate(picked_value(t, pick_t)):
        text[j] = rows


def attend_kernel(
    flags,
    r,
    p,
    text,
    pick_o,
    pick_t,
    lines,
    wo,
    wt,
    acc_x,
    acc_g,
    acc_f,
    acc_p,
    acc_t,
    q_gain,
    k_gain,
    bias,
    att,
    keep,
    even_t,
    odd_t,
    keys,
):
    n = 4 * ROWS
    mine = acc_x[...] + project(r, wt, KVQ, at=OWN)
    d_att = (acc_g[...] + project(r, wt, LAST, at=GIVEN)).astype(BF16)
    behind = acc_f[...] + project(r, wt, KV, at=BEHIND)
    beside = acc_p[...] + project(p, wt, KV, part_order(flags))
    words = acc_t[...] + project(text, wt, KV)
    t = text_rows(lines, wt)
    more = project(picked_value(t, pick_o), wo, KV) + project(picked_value(t, pick_t), wt, KV)
    high = mine[:, :W].astype(BF16)
    keep[KRAW, :W] = high
    keep[KRAW, W:] = (mine[:, :W] - high.astype(F32)).astype(BF16)
    keep[D_Q, W:] = jnp.zeros((ROWS, W), BF16)
    low = 0
    for values in (mine, beside[:ROWS], behind, beside[ROWS:], words, more):
        high = low + values.shape[0]
        for h in range(NH):
            kn = norm_rows(values[:, head(h)], k_gain[:, head(h)])
            keys[low:high, head(h)] = kn.astype(BF16)
        keys[low:high, W:] = values[:, W : 2 * W].astype(BF16)
        low = high
    even = flags[0].astype(F32)
    odd = 1.0 - even
    for h in range(NH):
        q = mine[:, val(NH + h)]
        qh = norm_rows(q, q_gain[:, head(h)]).astype(BF16)
        dh = d_att[:, head(h)]
        kh = keys[:, head(h)]
        vh = keys[:, val(h)]
        s = dot(qh, kh, NT) * SCALE + bias[...]
        e = jnp.exp(s - jnp.max(s, axis=-1, keepdims=True))
        p_h = e * (1.0 / jnp.sum(e, axis=-1, keepdims=True))
        pb = p_h.astype(BF16)
        att[:, head(h)] = dot(pb, vh).astype(BF16)
        dp = dot(dh, vh, NT)
        ds = (p_h * (dp - jnp.sum(p_h * dp, axis=-1, keepdims=True))).astype(BF16)
        d_q = dot(ds, kh) * SCALE
        keep[D_Q, head(h)] = norm_pull(q, q_gain[:, head(h)], d_q).astype(BF16)
        kt = dot(ds[:, :n], qh, TN) * SCALE
        vt = dot(pb[:, :n], dh, TN)
        for lanes, term in ((head(h), kt), (val(h), vt)):
            keep[: 2 * ROWS, lanes] = term[: 2 * ROWS].astype(BF16)
            even_t[:, lanes] = (term[2 * ROWS :] * even).astype(BF16)
            odd_t[:, lanes] = (term[2 * ROWS :] * odd).astype(BF16)


def out_kernel(att, wo, wt, pick_o, pick_t, out):
    for j in range(4):
        rows = slice(j * PART, (j + 1) * PART)
        o = dot(att[...], wo[rows, LAST], NT).astype(BF16)
        t = dot(att[...], wt[rows, LAST], NT).astype(BF16)
        out[j] = (dot(o, pick_o[...], NT) + dot(t, pick_t[...], NT)).astype(BF16)


def turn_kernel(flags, keep, got_even, got_odd, own, to_next, to_mate):
    total = keep[: 2 * ROWS, :].astype(F32) + got_even[...].astype(F32) + got_odd[...].astype(F32)
    own[...] = total[:ROWS]
    mate = flags[1].astype(F32)
    to_next[...] = (total[ROWS:] * (1.0 - mate)).astype(BF16)
    to_mate[...] = (total[ROWS:] * mate).astype(BF16)


def grad_kernel(own, from_next, from_mate, keep, k_gain, wo, wt, pick_o, pick_t, out):
    total = own[...] + from_next[...].astype(F32) + from_mate[...].astype(F32)
    kraw = keep[KRAW, :W].astype(F32) + keep[KRAW, W:].astype(F32)
    parts = [
        norm_pull(kraw[:, head(h)], k_gain[:, head(h)], total[:, head(h)]).astype(BF16)
        for h in range(NH)
    ]
    d = jnp.concatenate(parts + [total[:, W:].astype(BF16), keep[D_Q, :W]], axis=1)
    for j in range(4):
        rows = slice(j * PART, (j + 1) * PART)
        o = dot(d, wo[rows, KVQ], NT).astype(BF16)
        t = dot(d, wt[rows, KVQ], NT).astype(BF16)
        out[j] = (dot(o, pick_o[...], NT) + dot(t, pick_t[...], NT)).astype(BF16)


def head_total(parts):
    return f32_sum(*[parts[n] for n in range(4)]).astype(BF16)


def f32_sum(*terms):
    total = terms[0].astype(F32)
    for term in terms[1:]:
        total = total + term.astype(F32)
    return total


def head_shift(value, by):
    return lax.ppermute(value, "heads", [(i, (i + by) % 4) for i in range(4)])


def per_device(
    x_tiles, x_text, w_query, w_key, w_value, w_output, q_gain, k_gain, text_mask, windows, grad_out
):
    place = lax.axis_index("seq")
    me = lax.axis_index("heads")
    core, x, col = place & 1, place >> 5, place & 31
    window = lax.dynamic_slice(windows, (place, jnp.int32(0)), (1, 2))
    use_even = (window[:, :1] == x) == ((x & 1) == 0)
    use_core = (window[:, 1:] == col) == (core == 0)
    q_gain = q_gain[None, :]
    k_gain = k_gain[None, :]
    blocks = [(me - by) & 3 for by in range(4)]
    flags = jnp.stack([use_even[0, 0].astype(jnp.int32), use_core[0, 0].astype(jnp.int32)] + blocks)

    at = jnp.arange(PART, dtype=jnp.int32)
    inner = at % BLOCK
    feature = lax.broadcasted_iota(jnp.int32, (W, PART), 0)

    def pick(which):
        natural = ((inner // 12 * 4 + at // BLOCK) * 2 + which) * 12 + inner % 12
        hit = (feature == natural[None, :]) & (inner < 48)[None, :]
        return hit.astype(BF16)

    pick_o, pick_t = pick(core), pick(1 - core)
    t = jnp.arange(HALF_TEXT // 4, dtype=jnp.int32)
    line = t // 8 * BLOCK + 48 + t % 8
    lines = (line[:, None] == jnp.arange(PART, dtype=jnp.int32)[None, :]).astype(BF16)
    t = jnp.arange(TEXT, dtype=jnp.int32)
    token = place_of(t // 32 % 4, t // 2 % 4, t // 8 % 4, (t // 128) ^ core) * 2 + t % 2
    valid = jnp.sum(jnp.where(t[:, None] == token[None, :], text_mask[:, None], 0), axis=0)
    bias = jnp.concatenate(
        [jnp.zeros((4 * ROWS,), F32), jnp.where(valid == 1, 0.0, -1e30).astype(F32)]
    )[None, :]

    quarter = lax.dynamic_slice(x_tiles, (jnp.int32(0), me * W), (ROWS, W))
    mine = jnp.concatenate([w_key, w_value, w_query, w_output], axis=1)
    four = over_zh(jnp.concatenate([mine, x_text], axis=0))
    behind = jnp.where(use_even, row_even(x_tiles), row_odd(x_tiles))
    side = jnp.where(use_core, core_mate(quarter), next_chip(quarter))
    side, behind = lax.optimization_barrier((side, behind))
    c_even, c_odd = row_even(side), row_odd(side)
    four, c_even, c_odd = lax.optimization_barrier((four, c_even, c_odd))
    corner = jnp.where(use_even, c_even, c_odd)
    beside = jnp.concatenate([side, corner])
    block = jnp.concatenate([four[:, :12].reshape(48, 1536), four[:, 12:].reshape(8, 1536)], axis=0)
    parts = [beside] + [head_shift(beside, by) for by in (1, 2, 3)]
    wo = over_xy(block).reshape(16 * BLOCK, 1536)
    r_o, r_t = call(pick_kernel, (shape((4, 3 * ROWS, PART), BF16),) * 2, "v" * 5)(
        x_tiles, grad_out, behind, pick_o, pick_t
    )
    p_o, p_t = call(pick_parts_kernel, (shape((4, 2 * ROWS, PART), BF16),) * 2, "v" * 6)(
        *parts, pick_o, pick_t
    )
    wo, r_o, r_t, p_o, p_t, lines, bias, flags = lax.optimization_barrier(
        (wo, r_o, r_t, p_o, p_t, lines, bias, flags)
    )
    wt = core_mate(wo)

    *accs, text = call(
        first_kernel,
        (
            shape((ROWS, 3 * W), F32),
            shape((ROWS, W), F32),
            shape((ROWS, 2 * W), F32),
            shape((2 * ROWS, 2 * W), F32),
            shape((HALF_TEXT, 2 * W), F32),
            shape((4, HALF_TEXT, PART), BF16),
        ),
        "s" + "v" * 6,
    )(flags, r_o, p_o, pick_o, pick_t, lines, wo)
    att, keep, *terms = call(
        attend_kernel,
        (
            shape((ROWS, W), BF16),
            shape((4 * ROWS, 2 * W), BF16),
            *[shape((2 * ROWS, 2 * W), BF16)] * 2,
        ),
        "s" + "v" * 16,
        scratch=[pltpu.VMEM((1024, 768), BF16)],
        mib=28,
    )(flags, r_t, p_t, text, pick_o, pick_t, lines, wo, wt, *accs, q_gain, k_gain, bias)

    out = call(out_kernel, shape((4, ROWS, W), BF16), "v" * 5, flops=OUT_COST)(
        att, wo, wt, pick_o, pick_t
    )
    outs = lax.all_to_all(out, "heads", 0, 0)

    even_t, odd_t = terms
    own, to_next, to_mate = call(
        turn_kernel,
        (shape((ROWS, 2 * W), F32), *[shape((ROWS, 2 * W), BF16)] * 2),
        "svvv",
        mib=8,
        flops=TURN_COST,
    )(flags, keep, row_even(even_t), row_odd(odd_t))
    grad = call(grad_kernel, shape((4, ROWS, W), BF16), "v" * 9, flops=GRAD_COST)(
        own, next_chip(to_next), core_mate(to_mate), keep, k_gain, wo, wt, pick_o, pick_t
    )
    grads = lax.all_to_all(grad, "heads", 0, 0)
    return (head_total(outs), head_total(grads))


def solution(mesh):
    in_specs = (
        P("seq", None),
        P("seq", None),
        P("seq", "heads"),
        P("seq", "heads"),
        P("seq", "heads"),
        P("seq", "heads"),
        P("heads"),
        P("heads"),
        P(),
        P(),
        P("seq", None),
    )
    out_specs = (P("seq", "heads"), P("seq", "heads"))
    return jax.shard_map(
        per_device, mesh=mesh, in_specs=in_specs, out_specs=out_specs, check_vma=False
    )
```
